128 devices in a mesh: ctx: 16 (over z, x), tp: 8 (over y, core).
Axes of the slice: x: 4, y: 4, z: 4, core: 2. Of those that a mesh axis runs over, the one named last changes fastest.
Arguments:
- projected: bfloat16 [3, 4096, 8192], P(None, 'ctx', 'tp'), may hold values from -6 to 6
- feat_weight: float32 [3, 3, 8192], P(None, None, 'tp'), may hold values from -3.5 to 3.5
- long_filter: float32 [128, 8192], P(None, 'tp'), may hold values from -0.5 to 0.5
- out_weight: bfloat16 [8192, 6144], P('tp', 'ctx'), may hold values from -0.0625 to 0.0625
- seg_lengths: int32 [32], replicated, may hold values from 1 to 512, 4096 in all
- cotangent: bfloat16 [4096, 6144], P(('ctx', 'tp')), may hold values from -6 to 6
Outputs:
- block_out: bfloat16 [4096, 6144], P(('ctx', 'tp'))
- grad_projected: bfloat16 [3, 4096, 8192], P(None, 'ctx', 'tp')
- grad_long_filter: float32 [128, 8192], P(None, 'tp')
- grad_short_filter: float32 [3, 3, 8192], P(None, None, 'tp')
The draws below stay inside these ranges and needn't reach their ends.
Inputs may be any that keep to these rules, and one draw needn't show every extreme that they name: `seg_lengths`: lengths of the 32 packed segments; they sum to 4096, and the longest is exactly 512.
All inputs are finite; a program needn't handle non-finite values.
Results may differ from the reference program's by a relative error of at most 0.02.
Values may be sent and summed in bfloat16 or wider, within the bound.
A program may use at most 192 MiB of HBM per device.

```python
import math
import jax
import jax.numpy as jnp
import numpy as np
from jax import lax

D = 8192
OUTW = 6144
SHORT = 3
LONG = 128
NSEG = 32
TOKENS = 4096
N_TP = 8


def level_of(stream_key, shape, split, least, top_value):
    loudness = 1.0
    for axis_at, parts in split:
        steps = jax.random.uniform(jax.random.fold_in(jax.random.fold_in(stream_key, 6), axis_at), (parts,), jnp.float32, least / len(split), top_value / len(split))
        loudness = loudness * jnp.repeat(jnp.exp(steps), shape[axis_at] // parts).reshape((-1,) + (1,) * (len(shape) - 1 - axis_at))
    return loudness


def profile(amount, total, reach, skew):
    weights = [(1 << 20) // math.isqrt(standing ** skew) + 1 for standing in range(2, amount + 1)]
    rest, counts = total - reach - (amount - 1), [1] * (amount - 1)
    while rest > 0:
        candidates = [i for i in range(amount - 1) if counts[i] < reach]
        mass, left = sum([weights[i] for i in candidates]), rest
        for i in candidates:
            extra = min(reach - counts[i], max(1, left * weights[i] // mass), rest)
            counts[i] = counts[i] + extra
            rest = rest - extra
    return np.array([reach] + counts)


def ragged_sizes(rng, amount, total, most, slope):
    if amount == 2:
        one = jax.random.randint(rng, (), max(1, total - most), min(most, total - 1) + 1)
        return jnp.stack([one, total - one])
    tallies = jnp.asarray(profile(amount, total, most, slope), jnp.int32)
    couples = (amount - 1) // 2
    source_of, receiver = tallies[1:1 + 2 * couples:2], tallies[2:2 + 2 * couples:2]
    room = jnp.minimum(source_of - 1, most - receiver)
    shifted = jax.random.randint(jax.random.fold_in(rng, 1), (couples,), 0, 1 << 20) % (room + 1)
    tallies = tallies.at[1:1 + 2 * couples:2].set(source_of - shifted).at[2:2 + 2 * couples:2].set(receiver + shifted)
    return tallies[jax.random.permutation(jax.random.fold_in(rng, 2), amount)]


def normal_values(stream_key, shape, spread, reach, pieces=(), kind=jnp.bfloat16):
    loudness = level_of(stream_key, shape, pieces, -0.22, 0.18) if pieces else 1.0
    entries = jax.random.normal(stream_key, shape, jnp.float32) * spread * loudness
    return jnp.minimum(jnp.maximum(entries, -reach), reach).astype(kind)


def setup_inputs(seed: int = 0) -> dict:
    streams_of = jax.random.split(jax.random.key(seed), 7)
    projected = normal_values(streams_of[0], (3, TOKENS, D), 1.0, 6.0, ((1, 16), (2, 8)))
    feat_weight = normal_values(streams_of[1], (3, SHORT, D), SHORT ** -0.5, 3.5, ((2, 8),), jnp.float32)
    long_filter = normal_values(streams_of[2], (LONG, D), LONG ** -0.5, 0.5, ((1, 8),), jnp.float32)
    out_weight = normal_values(streams_of[3], (D, OUTW), D ** -0.5, 0.0625, ((0, 8), (1, 16)))
    seg_lengths = ragged_sizes(streams_of[4], NSEG, TOKENS, TOKENS // 8, 1).astype(jnp.int32)
    cotangent = normal_values(streams_of[5], (TOKENS, OUTW), 1.0, 6.0, ((0, 128),))
    return dict(projected=projected, feat_weight=feat_weight, long_filter=long_filter, out_weight=out_weight, seg_lengths=seg_lengths, cotangent=cotangent)


def segment_ages(positions, seg_lengths):
    seg_starts = jnp.cumsum(seg_lengths) - seg_lengths
    earlier = jnp.where(seg_starts[None, :] <= positions[:, None], seg_starts[None, :], 0)
    return (positions - jnp.max(earlier, axis=1)).astype(jnp.int32)


def causal_mix(source, weights, seg_age, extent):
    count_out = seg_age.shape[0]
    running = jnp.zeros((count_out, source.shape[1]), jnp.float32)
    for offset in range(extent):
        window = source[extent - 1 - offset: extent - 1 - offset + count_out].astype(jnp.float32)
        running = running + jnp.where((seg_age >= offset)[:, None], weights[offset][None, :] * window, 0.0)
    return running


def anticausal_mix(source, weights, later_age, extent, count_out):
    running = jnp.zeros((count_out, source.shape[1]), jnp.float32)
    for offset in range(extent):
        window = source[offset: offset + count_out].astype(jnp.float32)
        allowed = later_age[offset: offset + count_out] >= offset
        running = running + jnp.where(allowed[:, None], weights[offset][None, :] * window, 0.0)
    return running


def correlate(gradient, history, seg_age, extent):
    count_out = seg_age.shape[0]
    results = []
    for offset in range(extent):
        window = history[extent - 1 - offset: extent - 1 - offset + count_out].astype(jnp.float32)
        results.append(jnp.sum(jnp.where((seg_age >= offset)[:, None], gradient.astype(jnp.float32) * window, 0.0), axis=0))
    return jnp.stack(results)


def reference(projected, feat_weight, long_filter, out_weight, seg_lengths, cotangent):
    seg_age = segment_ages(jnp.arange(TOKENS, dtype=jnp.int32), seg_lengths)
    later_age = segment_ages(jnp.arange(TOKENS + LONG - 1, dtype=jnp.int32), seg_lengths)
    block_width = math.gcd(D, 512)
    block_count = D // block_width

    def blocks(array):
        shaped = array.reshape(array.shape[:-1] + (block_count, block_width))
        return jnp.moveaxis(shaped, -2, 0)

    def unblock(array):
        moved = jnp.moveaxis(array, 0, -2)
        return moved.reshape(moved.shape[:-2] + (D,))

    def forward_part(inputs, short_taps, long_taps):
        padded = jnp.pad(inputs, ((0, 0), (SHORT - 1, 0), (0, 0)))
        feats = jnp.stack([causal_mix(padded[branch], short_taps[branch], seg_age, SHORT) for branch in range(3)])
        product = (feats[1] * feats[2]).astype(jnp.bfloat16)
        product_ext = jnp.pad(product, ((LONG - 1, 0), (0, 0)))
        filtered = causal_mix(product_ext, long_taps, seg_age, LONG)
        gated = (feats[0] * filtered).astype(jnp.bfloat16)
        return padded, feats, product_ext, filtered, gated

    def forward_only(packed):
        return forward_part(packed[0], packed[1], packed[2])[4]

    gated = unblock(lax.map(forward_only, (blocks(projected), blocks(feat_weight), blocks(long_filter))))
    share = D // N_TP
    summed = jnp.zeros((TOKENS, OUTW), jnp.float32)
    for group in range(N_TP):
        partial_out = jnp.dot(gated[:, group * share:(group + 1) * share], out_weight[group * share:(group + 1) * share], preferred_element_type=jnp.float32).astype(jnp.bfloat16)
        partial_out = lax.optimization_barrier(partial_out)
        summed = summed + partial_out.astype(jnp.float32)
    block_out = summed.astype(jnp.bfloat16)
    grad_gated = lax.dot_general(cotangent, out_weight, (((1,), (1,)), ((), ())), preferred_element_type=jnp.float32).astype(jnp.bfloat16)

    def backward_part(packed):
        inputs, short_taps, long_taps, grad_in = packed
        padded, feats, product_ext, filtered, gated_again = forward_part(inputs, short_taps, long_taps)
        grad_long = (grad_in * feats[0]).astype(jnp.bfloat16)
        grad_query = grad_in.astype(jnp.float32) * filtered
        grad_product = anticausal_mix(jnp.pad(grad_long, ((0, LONG - 1), (0, 0))), long_taps, later_age, LONG, TOKENS)
        grad_taps = correlate(grad_long, product_ext, seg_age, LONG)
        grad_feats = jnp.stack([grad_query, grad_product * feats[2], grad_product * feats[1]])
        grad_ext = jnp.pad(grad_feats, ((0, 0), (0, SHORT - 1), (0, 0)))
        grad_inputs = jnp.stack([anticausal_mix(grad_ext[branch], short_taps[branch], later_age[:TOKENS + SHORT - 1], SHORT, TOKENS) for branch in range(3)]).astype(jnp.bfloat16)
        grad_short = jnp.stack([correlate(grad_feats[branch], padded[branch], seg_age, SHORT) for branch in range(3)])
        return grad_inputs, grad_taps, grad_short

    results = lax.map(backward_part, (blocks(projected), blocks(feat_weight), blocks(long_filter), blocks(grad_gated)))
    norm_factor = TOKENS ** -0.5
    return block_out, unblock(results[0]), unblock(results[1]) * norm_factor, unblock(results[2]) * norm_factor
```

```python
import functools
import math

import jax
import jax.numpy as jnp
import numpy as np
from jax import lax
from jax.experimental import pallas as pl
from jax.experimental.pallas import tpu as pltpu
from jax.sharding import PartitionSpec as P

F32 = jnp.float32
BF16 = jnp.bfloat16
ROWS = 256
CH = 1024
LB = CH // 128
BLK = 16
FAR = 8
TOKENS = 4096
NSEG = 32
PAD = 16


def tables():
    turn = np.pi * (2 * np.arange(BLK) + 1) / (2 * BLK)

    def wave(at):
        return np.concatenate([np.cos(np.outer(turn, at)), -np.sin(np.outer(turn, at))])

    into = wave(np.arange(BLK))
    back = wave(np.arange(BLK) + BLK) / BLK
    back[BLK:] = -back[BLK:]
    taps = np.zeros((FAR * 2 * BLK, FAR * BLK))
    window = wave(np.arange(2 * BLK))
    for k in range(FAR):
        for d in range(1, 2 * BLK):
            if k * BLK + d < FAR * BLK:
                taps[k * 2 * BLK : (k + 1) * 2 * BLK, k * BLK + d] = window[:, d]
    each = np.eye(FAR)
    stack = np.stack([np.kron(each, into), np.kron(each, back), taps])
    return stack.astype(jnp.bfloat16), np.swapaxes(stack, 1, 2).astype(jnp.bfloat16)


def lanes(l):
    return pl.ds(pl.multiple_of(l * 128, 128), 128)


def rows_at(start, count):
    return pl.ds(pl.multiple_of(start, 8), count)


def find_ages(seg_ref, base, age_ref, room_ref):
    def chunk(i, carry):
        at = rows_at(i * 64, 64)
        pos = lax.broadcasted_iota(jnp.int32, (64, 128), 0) + (base - 128 + i * 64)

        def one(k, state):
            start, latest, after = state
            end = start + seg_ref[k]
            inside = pos >= start
            return end, jnp.where(inside, start, latest), jnp.where(inside, end, after)

        zero = jnp.zeros((64, 128), jnp.int32)
        _, latest, after = lax.fori_loop(0, NSEG, one, (jnp.int32(0), zero, zero))
        age_ref[at, :] = jnp.where(pos < TOKENS, pos - latest, -1)
        room_ref[at, :] = after - pos
        return carry

    lax.fori_loop(0, 8, chunk, 0)


def in_block(count):
    return lax.rem(lax.broadcasted_iota(jnp.int32, (count, 128), 0), BLK)


def load_inputs(proj_ref, jhalo_ref, pj):
    def lane(l, carry):
        for b in range(3):
            pj[b, l, 0:PAD, :] = jhalo_ref[b, :, lanes(l)].astype(F32)
            pj[b, l, PAD : PAD + ROWS, :] = proj_ref[b, :, lanes(l)].astype(F32)
        return carry

    lax.fori_loop(0, LB, lane, 0)


def features(pj, fw_ref, age_ref, room_ref, feats, xs, xv, prod, first, count):
    def step(at, carry):
        l, r0 = at // count, (first + at % count) * 64
        age = age_ref[rows_at(128 + r0, 64), :]
        inside = in_block(64)
        got = []
        for b in range(3):
            total = pj[b, l, rows_at(PAD + r0, 64), :] * fw_ref[b, 0:1, lanes(l)]
            for i in range(1, 3):
                window = pj[b, l, pl.ds(PAD + r0 - i, 64), :]
                total = total + jnp.where(age >= i, window, 0.0) * fw_ref[b, i : i + 1, lanes(l)]
            feats[b, l, rows_at(r0, 64), :] = total
            got.append(total)
        product = (got[1] * got[2]).astype(BF16)
        wide = product.astype(F32)
        xs[l, rows_at(PAD + r0, 64), :] = wide
        live = room_ref[rows_at(128 + r0, 64), :] >= BLK - inside
        xv[pl.ds(pl.multiple_of(128 + r0, 16), 64), lanes(l)] = jnp.where(live, wide, 0.0).astype(BF16)
        if prod is not None:
            prod[pl.ds(pl.multiple_of(r0, 16), 64), lanes(l)] = product
        return carry

    lax.fori_loop(0, LB * count, step, 0)


def mask_halo(phalo_ref, room_ref, xv):
    def step(at, carry):
        l, r0 = at // 2, (at % 2) * 64
        live = room_ref[rows_at(r0, 64), :] >= BLK - in_block(64)
        rows = pl.ds(pl.multiple_of(r0, 16), 64)
        xv[rows, lanes(l)] = jnp.where(live, phalo_ref[rows, lanes(l)].astype(F32), 0.0).astype(BF16)
        return carry

    lax.fori_loop(0, LB * 2, step, 0)


def transform(table, source, target, group):
    def step(c, carry):
        cols = pl.ds(pl.multiple_of(c * 256, 256), 256)
        target[group * 256 : (group + 1) * 256, cols] = jnp.dot(
            table, source[group * 128 : (group + 1) * 128, cols], preferred_element_type=F32
        )
        return carry

    lax.fori_loop(0, CH // 256, step, 0)


def far_forward(spec_x, spec_g, age_ref, spec_y):
    def outer(at, carry):
        l, ft = at // 2, at % 2
        g = [
            (spec_g[rows_at(k * 32 + ft * 8, 8), lanes(l)], spec_g[rows_at(k * 32 + 16 + ft * 8, 8), lanes(l)])
            for k in range(FAR)
        ]

        def inner(m, carry):
            reach = age_ref[pl.ds(128 + m * BLK - 1, 1), :]
            reach = jnp.broadcast_to(reach, (8, 128))
            re = jnp.zeros((8, 128), F32)
            im = jnp.zeros((8, 128), F32)
            for k in range(1, FAR + 1):
                live = reach >= BLK * (k - 1)
                base = (FAR + m - k) * 32 + ft * 8
                xr = jnp.where(live, spec_x[rows_at(base, 8), lanes(l)], 0.0)
                xi = jnp.where(live, spec_x[rows_at(base + 16, 8), lanes(l)], 0.0)
                gr, gi = g[k - 1]
                re = re + (gr * xr - gi * xi)
                im = im + (gr * xi + gi * xr)
            spec_y[rows_at(m * 32 + ft * 8, 8), lanes(l)] = re
            spec_y[rows_at(m * 32 + 16 + ft * 8, 8), lanes(l)] = -im
            return carry

        lax.fori_loop(0, ROWS // BLK, inner, 0)
        return carry

    lax.fori_loop(0, LB * 2, outer, 0)


def far_back(spec_z, spec_g, age_ref, spec_p):
    def outer(at, carry):
        l, ft = at // 2, at % 2
        g = [
            (spec_g[rows_at(k * 32 + ft * 8, 8), lanes(l)], spec_g[rows_at(k * 32 + 16 + ft * 8, 8), lanes(l)])
            for k in range(FAR)
        ]

        def inner(n, carry):
            re = jnp.zeros((8, 128), F32)
            im = jnp.zeros((8, 128), F32)
            for k in range(1, FAR + 1):
                reach = age_ref[pl.ds(128 + (n + k) * BLK - 1, 1), :]
                live = jnp.broadcast_to(reach, (8, 128)) >= BLK * (k - 1)
                base = (n + k) * 32 + ft * 8
                zr = jnp.where(live, spec_z[rows_at(base, 8), lanes(l)], 0.0)
                zi = jnp.where(live, spec_z[rows_at(base + 16, 8), lanes(l)], 0.0)
                gr, gi = g[k - 1]
                re = re + (gr * zr - gi * zi)
                im = im + (gr * zi + gi * zr)
            spec_p[rows_at(n * 32 + ft * 8, 8), lanes(l)] = re
            spec_p[rows_at(n * 32 + 16 + ft * 8, 8), lanes(l)] = -im
            return carry

        lax.fori_loop(0, ROWS // BLK, inner, 0)
        return carry

    lax.fori_loop(0, LB * 2, outer, 0)


def far_taps(spec_x, spec_z, age_ref, spec_q):
    def outer(at, carry):
        l, ft = at // 2, at % 2

        def inner(m, state):
            reach = jnp.broadcast_to(age_ref[pl.ds(128 + m * BLK - 1, 1), :], (8, 128))
            zr = spec_z[rows_at(m * 32 + ft * 8, 8), lanes(l)]
            zi = spec_z[rows_at(m * 32 + 16 + ft * 8, 8), lanes(l)]
            out = []
            for k in range(1, FAR + 1):
                live = reach >= BLK * (k - 1)
                base = (FAR + m - k) * 32 + ft * 8
                xr = jnp.where(live, spec_x[rows_at(base, 8), lanes(l)], 0.0)
                xi = jnp.where(live, spec_x[rows_at(base + 16, 8), lanes(l)], 0.0)
                re, im = state[2 * k - 2], state[2 * k - 1]
                out.append(re + (xr * zr - xi * zi))
                out.append(im + (xr * zi + xi * zr))
            return tuple(out)

        zero = jnp.zeros((8, 128), F32)
        state = lax.fori_loop(0, ROWS // BLK, inner, (zero,) * (2 * FAR))
        for k in range(FAR):
            spec_q[rows_at(k * 32 + ft * 8, 8), lanes(l)] = state[2 * k]
            spec_q[rows_at(k * 32 + 16 + ft * 8, 8), lanes(l)] = -state[2 * k + 1]
        return carry

    lax.fori_loop(0, LB * 2, outer, 0)


def inverse(table, source, target, groups):
    def step(c, carry):
        cols = pl.ds(pl.multiple_of(c * 256, 256), 256)
        for group in range(groups):
            target[group * 128 : (group + 1) * 128, cols] = jnp.dot(
                table, source[group * 256 : (group + 1) * 256, cols].astype(BF16), preferred_element_type=F32
            )
        return carry

    lax.fori_loop(0, CH // 256, step, 0)


def near_forward(xs, lf_ref, age_ref, wide, feats, filt, gated):
    def step(at, carry):
        l, r0 = at // 4, (at % 4) * 64
        age = age_ref[rows_at(128 + r0, 64), :]
        inside = in_block(64)
        near = jnp.minimum(age, inside)
        total = jnp.where(age > inside, wide[rows_at(r0, 64), lanes(l)], 0.0)
        for j in range(BLK):
            window = xs[l, pl.ds(PAD + r0 - j, 64), :]
            total = total + jnp.where(near >= j, window, 0.0) * lf_ref[j : j + 1, lanes(l)]
        filt[l, rows_at(r0, 64), :] = total
        gate = feats[0, l, rows_at(r0, 64), :] * total
        gated[pl.ds(pl.multiple_of(r0, 16), 64), lanes(l)] = gate.astype(BF16)
        return carry

    lax.fori_loop(0, LB * 4, step, 0)


def make_long(gg_ref, feats, age_ref, gs_, gv, first, count):
    def step(at, carry):
        l, r0 = at // count, (first + at % count) * 64
        rows = pl.ds(pl.multiple_of(r0, 16), 64)
        long = (gg_ref[rows, lanes(l)].astype(F32) * feats[0, l, rows_at(r0, 64), :]).astype(BF16).astype(F32)
        gs_[l, rows_at(r0, 64), :] = long
        live = age_ref[rows_at(128 + r0, 64), :] > in_block(64)
        gv[rows, lanes(l)] = jnp.where(live, long, 0.0).astype(BF16)
        return carry

    lax.fori_loop(0, LB * count, step, 0)


def mask_next(glhalo_ref, age_ref, gv):
    def step(at, carry):
        l, r0 = at // 2, (at % 2) * 64
        live = age_ref[rows_at(128 + ROWS + r0, 64), :] > in_block(64)
        long = glhalo_ref[pl.ds(pl.multiple_of(r0, 16), 64), lanes(l)].astype(F32)
        gv[pl.ds(pl.multiple_of(ROWS + r0, 16), 64), lanes(l)] = jnp.where(live, long, 0.0).astype(BF16)
        return carry

    lax.fori_loop(0, LB * 2, step, 0)


def near_back(gs_, xs, lf_ref, age_ref, room_ref, wide, gg_ref, filt, feats, gf, near_taps):
    def lane(l, carry):
        def step(i, sums):
            r0 = i * 64
            age = age_ref[rows_at(128 + r0, 64), :]
            room = room_ref[rows_at(128 + r0, 64), :]
            inside = in_block(64)
            near = jnp.minimum(age, inside)
            ahead = jnp.minimum(room, BLK - inside)
            here = gs_[l, rows_at(r0, 64), :]
            total = jnp.where(room >= BLK - inside, wide[rows_at(r0, 64), lanes(l)], 0.0)
            out = []
            for j in range(BLK):
                later = gs_[l, pl.ds(r0 + j, 64), :]
                total = total + jnp.where(ahead > j, later, 0.0) * lf_ref[j : j + 1, lanes(l)]
                window = xs[l, pl.ds(PAD + r0 - j, 64), :]
                both = jnp.where(near >= j, window, 0.0) * here
                out.append(sums[j] + jnp.sum(both.reshape(8, 8, 128), axis=0))
            grad = gg_ref[pl.ds(pl.multiple_of(r0, 16), 64), lanes(l)].astype(F32)
            gf[0, l, rows_at(r0, 64), :] = grad * filt[l, rows_at(r0, 64), :]
            gf[1, l, rows_at(r0, 64), :] = total * feats[2, l, rows_at(r0, 64), :]
            gf[2, l, rows_at(r0, 64), :] = total * feats[1, l, rows_at(r0, 64), :]
            return tuple(out)

        sums = lax.fori_loop(0, 4, step, (jnp.zeros((8, 128), F32),) * BLK)
        for j in range(BLK):
            near_taps[j : j + 1, lanes(l)] = jnp.sum(sums[j], axis=0, keepdims=True)
        return carry

    lax.fori_loop(0, LB, lane, 0)


def last_step(gf, pj, fw_ref, age_ref, room_ref, gproj_ref, short_ref):
    def lane(l, carry):
        def step(i, sums):
            r0 = i * 64
            age = age_ref[rows_at(128 + r0, 64), :]
            room = room_ref[rows_at(128 + r0, 64), :]
            out = []
            for b in range(3):
                here = gf[b, l, rows_at(r0, 64), :]
                total = here * fw_ref[b, 0:1, lanes(l)]
                for i_tap in range(3):
                    window = pj[b, l, pl.ds(PAD + r0 - i_tap, 64), :]
                    if i_tap:
                        later = gf[b, l, pl.ds(r0 + i_tap, 64), :]
                        total = total + jnp.where(room > i_tap, later, 0.0) * fw_ref[b, i_tap : i_tap + 1, lanes(l)]
                        window = jnp.where(age >= i_tap, window, 0.0)
                    out.append(sums[b * 3 + i_tap] + jnp.sum((here * window).reshape(8, 8, 128), axis=0))
                gproj_ref[b, pl.ds(pl.multiple_of(r0, 16), 64), lanes(l)] = total.astype(BF16)
            return tuple(out)

        sums = lax.fori_loop(0, 4, step, (jnp.zeros((8, 128), F32),) * 9)
        for at in range(9):
            short_ref[at : at + 1, lanes(l)] = jnp.sum(sums[at], axis=0, keepdims=True)
        return carry

    lax.fori_loop(0, LB, lane, 0)


def kernel_forward(
    base_ref, seg_ref, proj_ref, jhalo_ref, phalo_ref, fw_ref, lf_ref, tab_ref, tabt_ref,
    gated, feats, filt, spec_x, spec_g, xs, pj, age_ref, room_ref, xv, spec_y, wide, lfb,
):
    find_ages(seg_ref, base_ref[0], age_ref, room_ref)
    load_inputs(proj_ref, jhalo_ref, pj)
    xs[:, 0:PAD, :] = jnp.zeros((LB, PAD, 128), F32)
    features(pj, fw_ref, age_ref, room_ref, feats, xs, xv, None, 0, 4)
    mask_halo(phalo_ref, room_ref, xv)
    lfb[...] = lf_ref[...].astype(BF16)
    transform(tab_ref[2], lfb, spec_g, 0)
    for group in range(3):
        transform(tab_ref[0], xv, spec_x, group)
    far_forward(spec_x, spec_g, age_ref, spec_y)
    inverse(tabt_ref[1], spec_y, wide, 2)
    near_forward(xs, lf_ref, age_ref, wide, feats, filt, gated)


def kernel_back(
    gg_ref, glhalo_ref, lf_ref, tab_ref, tabt_ref, feats, filt, spec_x, spec_g, xs, age_ref, room_ref,
    gf, taps_ref, gs_, gv, spec_z, spec_p, spec_q, wide, near_taps,
):
    make_long(gg_ref, feats, age_ref, gs_, gv, 0, 4)
    gs_[:, ROWS : ROWS + PAD, :] = jnp.zeros((LB, PAD, 128), F32)
    mask_next(glhalo_ref, age_ref, gv)
    for group in range(3):
        transform(tab_ref[1], gv, spec_z, group)
    far_back(spec_z, spec_g, age_ref, spec_p)
    inverse(tabt_ref[0], spec_p, wide, 2)
    far_taps(spec_x, spec_z, age_ref, spec_q)
    near_back(gs_, xs, lf_ref, age_ref, room_ref, wide, gg_ref, filt, feats, gf, near_taps)
    inverse(tabt_ref[2], spec_q, taps_ref, 1)
    taps_ref[0:BLK, :] = taps_ref[0:BLK, :] + near_taps[...]


def kernel_last(gf_ref, gfhalo_ref, pj, fw_ref, age_ref, room_ref, gproj_ref, short_ref, gf):
    gf[:, :, 0:ROWS, :] = gf_ref[...]
    gf[:, :, ROWS : ROWS + 8, :] = gfhalo_ref[...]
    last_step(gf, pj, fw_ref, age_ref, room_ref, gproj_ref, short_ref)


def call(kernel, outs, scratch, smem, args):
    vm = pl.BlockSpec(memory_space=pltpu.VMEM)
    sm = pl.BlockSpec(memory_space=pltpu.SMEM)
    return pl.pallas_call(
        kernel,
        out_shape=[jax.ShapeDtypeStruct(s, d) for s, d in outs],
        in_specs=[sm] * smem + [vm] * (len(args) - smem),
        out_specs=[vm] * len(outs),
        scratch_shapes=[pltpu.VMEM(s, d) for s, d in scratch],
        compiler_params=pltpu.CompilerParams(vmem_limit_bytes=56 * 2**20),
    )(*args)


SPEC = ((3 * 256, CH), F32)
AGE = ((512, 128), jnp.int32)
LANED = ((LB, ROWS, 128), F32)


def forward_call(base, seg, proj, jhalo, phalo, fw, lf, tab, tabt):
    return call(
        kernel_forward,
        [((ROWS, CH), BF16), ((3,) + LANED[0], F32), LANED, SPEC, ((256, CH), F32),
         ((LB, PAD + ROWS, 128), F32), ((3, LB, PAD + ROWS, 128), F32), AGE, AGE],
        [((128 + ROWS, CH), BF16), ((512, CH), F32), ((ROWS, CH), F32), ((128, CH), BF16)],
        2,
        (base, seg, proj, jhalo, phalo, fw, lf, tab, tabt),
    )


def back_call(*args):
    return call(
        kernel_back,
        [((3,) + LANED[0], F32), ((128, CH), F32)],
        [((LB, ROWS + PAD, 128), F32), ((ROWS + 128, CH), BF16), SPEC, ((512, CH), F32), ((256, CH), F32),
         ((ROWS, CH), F32), ((BLK, CH), F32)],
        0,
        args,
    )


def last_call(*args):
    return call(
        kernel_last,
        [((3, ROWS, CH), BF16), ((9, CH), F32)],
        [((3, LB, ROWS + PAD, 128), F32)],
        0,
        args,
    )


def from_behind(x, axis, by):
    size = lax.axis_size(axis)
    pairs = [(i, i + by) for i in range(size) if 0 <= i + by < size]
    return lax.ppermute(x, axis, pairs)


def segment_ages(positions, seg_lengths):
    seg_starts = jnp.cumsum(seg_lengths) - seg_lengths
    earlier = jnp.where(seg_starts[None, :] <= positions[:, None], seg_starts[None, :], 0)
    return positions - jnp.max(earlier, axis=1)


def shards(projected, feat_weight, long_filter, out_weight, seg_lengths, cotangent):
    tab, tabt = (jnp.asarray(t) for t in tables())
    base = lax.axis_index("ctx") * ROWS
    cot_rows = lax.all_gather(cotangent, "tp", axis=0, tiled=True)
    weight = lax.all_gather(out_weight, "ctx", axis=1, tiled=True)
    jhalo = from_behind(projected[:, ROWS - 16 :, :], "ctx", 1)
    tail_age = segment_ages(base + 128 + jnp.arange(128, dtype=jnp.int32), seg_lengths)
    tail = []
    for b in (1, 2):
        total = 0.0
        for i in range(3):
            window = projected[b, 128 - i : 256 - i].astype(F32)
            total = total + jnp.where((tail_age >= i)[:, None], window * feat_weight[b, i][None, :], 0.0)
        tail.append(total)
    phalo = from_behind((tail[0] * tail[1]).astype(BF16), "ctx", 1)
    gated, feats, filt, spec_x, spec_g, xs, pj, age, room = forward_call(
        base.reshape(1), seg_lengths, projected, jhalo, phalo, feat_weight, long_filter, tab, tabt
    )
    grad_gated = lax.dot_general(cot_rows, weight, (((1,), (1,)), ((), ())), preferred_element_type=F32)
    grad_gated = grad_gated.astype(BF16)
    front = jnp.swapaxes(feats[0, :, :128, :], 0, 1).reshape(128, CH)
    glhalo = from_behind((grad_gated[:128] * front).astype(BF16), "ctx", -1)
    terms = jnp.dot(gated, weight, preferred_element_type=F32)
    summed = lax.psum_scatter(terms.astype(BF16), "tp", scatter_dimension=0, tiled=True)
    gf, taps = back_call(
        grad_gated, glhalo, long_filter, tab, tabt, feats, filt, spec_x, spec_g, xs, age, room
    )
    gfhalo = from_behind(gf[:, :, :8, :], "ctx", -1)
    grad_inputs, short = last_call(gf, gfhalo, pj, feat_weight, age, room)
    norm = TOKENS**-0.5
    both = jnp.concatenate([taps, jnp.pad(short, ((0, 7), (0, 0)))], axis=0).astype(BF16)
    both = lax.psum(both, "ctx").astype(F32) * norm
    return (summed, grad_inputs, both[:128], both[128:137].reshape(3, 3, CH))


def solution(mesh):
    return jax.shard_map(
        shards,
        mesh=mesh,
        in_specs=(
            P(None, "ctx", "tp"),
            P(None, None, "tp"),
            P(None, "tp"),
            P("tp", "ctx"),
            P(),
            P(("ctx", "tp"), None),
        ),
        out_specs=(
            P(("ctx", "tp"), None),
            P(None, "ctx", "tp"),
            P(None, "tp"),
            P(None, None, "tp"),
        ),
        check_vma=False,
    )
```

```python
import jax
import jax.numpy as jnp
import numpy as np
from jax import lax
from jax.experimental import pallas as pl
from jax.experimental.pallas import tpu as pltpu
from jax.sharding import PartitionSpec as P

F32 = jnp.float32
BF16 = jnp.bfloat16
ROWS = 256
CH = 1024
LB = CH // 128
BLK = 16
FAR = 8
TOKENS = 4096
NSEG = 32
PAD = 16


def tables():
    turn = np.pi * (2 * np.arange(BLK) + 1) / (2 * BLK)

    def wave(at):
        return np.concatenate([np.cos(np.outer(turn, at)), -np.sin(np.outer(turn, at))])

    into = wave(np.arange(BLK))
    back = wave(np.arange(BLK) + BLK) / BLK
    back[BLK:] = -back[BLK:]
    taps = np.zeros((FAR * 2 * BLK, FAR * BLK))
    window = wave(np.arange(2 * BLK))
    for k in range(FAR):
        for d in range(1, 2 * BLK):
            if k * BLK + d < FAR * BLK:
                taps[k * 2 * BLK : (k + 1) * 2 * BLK, k * BLK + d] = window[:, d]
    each = np.eye(FAR)
    stack = np.stack([np.kron(each, into), np.kron(each, back), taps])
    return stack.astype(jnp.bfloat16), np.swapaxes(stack, 1, 2).astype(jnp.bfloat16)


def lanes(l):
    return pl.ds(pl.multiple_of(l * 128, 128), 128)


def rows_at(start, count):
    return pl.ds(pl.multiple_of(start, 8), count)


def find_ages(seg_ref, base, age_ref, room_ref):
    def chunk(i, carry):
        at = rows_at(i * 64, 64)
        pos = lax.broadcasted_iota(jnp.int32, (64, 128), 0) + (base - 128 + i * 64)

        def one(k, state):
            start, latest, after = state
            end = start + seg_ref[k]
            inside = pos >= start
            return end, jnp.where(inside, start, latest), jnp.where(inside, end, after)

        zero = jnp.zeros((64, 128), jnp.int32)
        _, latest, after = lax.fori_loop(0, NSEG, one, (jnp.int32(0), zero, zero))
        age_ref[at, :] = jnp.where(pos < TOKENS, pos - latest, -1)
        room_ref[at, :] = after - pos
        return carry

    lax.fori_loop(0, 8, chunk, 0)


def in_block(count):
    return lax.rem(lax.broadcasted_iota(jnp.int32, (count, 128), 0), BLK)


def load_inputs(source, pj, first, count):
    def lane(l, carry):
        for b in range(3):
            pj[b, l, first : first + count, :] = source[b, :, lanes(l)].astype(F32)
        return carry

    lax.fori_loop(0, LB, lane, 0)


def features(pj, fw_ref, age_ref, room_ref, feats, xs, xv, prod, first, count):
    def step(at, carry):
        l, r0 = at // count, (first + at % count) * 64
        age = age_ref[rows_at(128 + r0, 64), :]
        inside = in_block(64)
        got = []
        for b in range(3):
            total = pj[b, l, rows_at(PAD + r0, 64), :] * fw_ref[b, 0:1, lanes(l)]
            for i in range(1, 3):
                window = pj[b, l, pl.ds(PAD + r0 - i, 64), :]
                total = total + jnp.where(age >= i, window, 0.0) * fw_ref[b, i : i + 1, lanes(l)]
            feats[b, l, rows_at(r0, 64), :] = total
            got.append(total)
        product = (got[1] * got[2]).astype(BF16)
        wide = product.astype(F32)
        xs[l, rows_at(PAD + r0, 64), :] = wide
        live = room_ref[rows_at(128 + r0, 64), :] >= BLK - inside
        xv[pl.ds(pl.multiple_of(128 + r0, 16), 64), lanes(l)] = jnp.where(live, wide, 0.0).astype(BF16)
        if first:
            prod[pl.ds(pl.multiple_of(r0 - 128, 16), 64), lanes(l)] = product
        return carry

    lax.fori_loop(0, LB * count, step, 0)


def mask_halo(phalo_ref, room_ref, xv):
    def step(at, carry):
        l, r0 = at // 2, (at % 2) * 64
        live = room_ref[rows_at(r0, 64), :] >= BLK - in_block(64)
        rows = pl.ds(pl.multiple_of(r0, 16), 64)
        xv[rows, lanes(l)] = jnp.where(live, phalo_ref[rows, lanes(l)].astype(F32), 0.0).astype(BF16)
        return carry

    lax.fori_loop(0, LB * 2, step, 0)


def transform(table, source, target, group):
    def step(c, carry):
        cols = pl.ds(pl.multiple_of(c * 256, 256), 256)
        target[group * 256 : (group + 1) * 256, cols] = jnp.dot(
            table, source[group * 128 : (group + 1) * 128, cols], preferred_element_type=F32
        )
        return carry

    lax.fori_loop(0, CH // 256, step, 0)


def far_forward(spec_x, spec_g, age_ref, spec_y):
    def outer(at, carry):
        l, ft = at // 2, at % 2
        g = [
            (spec_g[rows_at(k * 32 + ft * 8, 8), lanes(l)], spec_g[rows_at(k * 32 + 16 + ft * 8, 8), lanes(l)])
            for k in range(FAR)
        ]

        def inner(m, carry):
            reach = age_ref[pl.ds(128 + m * BLK - 1, 1), :]
            reach = jnp.broadcast_to(reach, (8, 128))
            re = jnp.zeros((8, 128), F32)
            im = jnp.zeros((8, 128), F32)
            for k in range(1, FAR + 1):
                live = reach >= BLK * (k - 1)
                base = (FAR + m - k) * 32 + ft * 8
                xr = jnp.where(live, spec_x[rows_at(base, 8), lanes(l)], 0.0)
                xi = jnp.where(live, spec_x[rows_at(base + 16, 8), lanes(l)], 0.0)
                gr, gi = g[k - 1]
                re = re + (gr * xr - gi * xi)
                im = im + (gr * xi + gi * xr)
            spec_y[rows_at(m * 32 + ft * 8, 8), lanes(l)] = re
            spec_y[rows_at(m * 32 + 16 + ft * 8, 8), lanes(l)] = -im
            return carry

        lax.fori_loop(0, ROWS // BLK, inner, 0)
        return carry

    lax.fori_loop(0, LB * 2, outer, 0)


def far_back(spec_z, spec_g, age_ref, spec_p):
    def outer(at, carry):
        l, ft = at // 2, at % 2
        g = [
            (spec_g[rows_at(k * 32 + ft * 8, 8), lanes(l)], spec_g[rows_at(k * 32 + 16 + ft * 8, 8), lanes(l)])
            for k in range(FAR)
        ]

        def inner(n, carry):
            re = jnp.zeros((8, 128), F32)
            im = jnp.zeros((8, 128), F32)
            for k in range(1, FAR + 1):
                reach = age_ref[pl.ds(128 + (n + k) * BLK - 1, 1), :]
                live = jnp.broadcast_to(reach, (8, 128)) >= BLK * (k - 1)
                base = (n + k) * 32 + ft * 8
                zr = jnp.where(live, spec_z[rows_at(base, 8), lanes(l)], 0.0)
                zi = jnp.where(live, spec_z[rows_at(base + 16, 8), lanes(l)], 0.0)
                gr, gi = g[k - 1]
                re = re + (gr * zr - gi * zi)
                im = im + (gr * zi + gi * zr)
            spec_p[rows_at(n * 32 + ft * 8, 8), lanes(l)] = re
            spec_p[rows_at(n * 32 + 16 + ft * 8, 8), lanes(l)] = -im
            return carry

        lax.fori_loop(0, ROWS // BLK, inner, 0)
        return carry

    lax.fori_loop(0, LB * 2, outer, 0)


def far_taps(spec_x, spec_z, age_ref, spec_q):
    def outer(at, carry):
        l, ft = at // 2, at % 2

        def inner(m, state):
            reach = jnp.broadcast_to(age_ref[pl.ds(128 + m * BLK - 1, 1), :], (8, 128))
            zr = spec_z[rows_at(m * 32 + ft * 8, 8), lanes(l)]
            zi = spec_z[rows_at(m * 32 + 16 + ft * 8, 8), lanes(l)]
            out = []
            for k in range(1, FAR + 1):
                live = reach >= BLK * (k - 1)
                base = (FAR + m - k) * 32 + ft * 8
                xr = jnp.where(live, spec_x[rows_at(base, 8), lanes(l)], 0.0)
                xi = jnp.where(live, spec_x[rows_at(base + 16, 8), lanes(l)], 0.0)
                re, im = state[2 * k - 2], state[2 * k - 1]
                out.append(re + (xr * zr - xi * zi))
                out.append(im + (xr * zi + xi * zr))
            return tuple(out)

        zero = jnp.zeros((8, 128), F32)
        state = lax.fori_loop(0, ROWS // BLK, inner, (zero,) * (2 * FAR))
        for k in range(FAR):
            spec_q[rows_at(k * 32 + ft * 8, 8), lanes(l)] = state[2 * k]
            spec_q[rows_at(k * 32 + 16 + ft * 8, 8), lanes(l)] = -state[2 * k + 1]
        return carry

    lax.fori_loop(0, LB * 2, outer, 0)


def inverse(table, source, target, groups):
    def step(c, carry):
        cols = pl.ds(pl.multiple_of(c * 256, 256), 256)
        for group in range(groups):
            target[group * 128 : (group + 1) * 128, cols] = jnp.dot(
                table, source[group * 256 : (group + 1) * 256, cols].astype(BF16), preferred_element_type=F32
            )
        return carry

    lax.fori_loop(0, CH // 256, step, 0)


def near_forward(xs, lf_ref, age_ref, wide, feats, filt, gated):
    def step(at, carry):
        l, r0 = at // 4, (at % 4) * 64
        age = age_ref[rows_at(128 + r0, 64), :]
        inside = in_block(64)
        near = jnp.minimum(age, inside)
        total = jnp.where(age > inside, wide[rows_at(r0, 64), lanes(l)], 0.0)
        for j in range(BLK):
            window = xs[l, pl.ds(PAD + r0 - j, 64), :]
            total = total + jnp.where(near >= j, window, 0.0) * lf_ref[j : j + 1, lanes(l)]
        filt[l, rows_at(r0, 64), :] = total
        gate = feats[0, l, rows_at(r0, 64), :] * total
        gated[pl.ds(pl.multiple_of(r0, 16), 64), lanes(l)] = gate.astype(BF16)
        return carry

    lax.fori_loop(0, LB * 4, step, 0)


def make_long(gg_ref, feats, age_ref, gs_, gl, gv, first, count):
    def step(at, carry):
        l, r0 = at // count, (first + at % count) * 64
        rows = pl.ds(pl.multiple_of(r0, 16), 64)
        sent = (gg_ref[rows, lanes(l)].astype(F32) * feats[0, l, rows_at(r0, 64), :]).astype(BF16)
        long = sent.astype(F32)
        if not first:
            gl[rows, lanes(l)] = sent
        gs_[l, rows_at(r0, 64), :] = long
        live = age_ref[rows_at(128 + r0, 64), :] > in_block(64)
        gv[rows, lanes(l)] = jnp.where(live, long, 0.0).astype(BF16)
        return carry

    lax.fori_loop(0, LB * count, step, 0)


def mask_next(glhalo_ref, age_ref, gv):
    def step(at, carry):
        l, r0 = at // 2, (at % 2) * 64
        live = age_ref[rows_at(128 + ROWS + r0, 64), :] > in_block(64)
        long = glhalo_ref[pl.ds(pl.multiple_of(r0, 16), 64), lanes(l)].astype(F32)
        gv[pl.ds(pl.multiple_of(ROWS + r0, 16), 64), lanes(l)] = jnp.where(live, long, 0.0).astype(BF16)
        return carry

    lax.fori_loop(0, LB * 2, step, 0)


def near_back(gs_, xs, lf_ref, age_ref, room_ref, wide, gg_ref, filt, feats, gf, near_taps):
    def lane(l, carry):
        def step(i, sums):
            r0 = i * 64
            age = age_ref[rows_at(128 + r0, 64), :]
            room = room_ref[rows_at(128 + r0, 64), :]
            inside = in_block(64)
            near = jnp.minimum(age, inside)
            ahead = jnp.minimum(room, BLK - inside)
            here = gs_[l, rows_at(r0, 64), :]
            total = jnp.where(room >= BLK - inside, wide[rows_at(r0, 64), lanes(l)], 0.0)
            out = []
            for j in range(BLK):
                later = gs_[l, pl.ds(r0 + j, 64), :]
                total = total + jnp.where(ahead > j, later, 0.0) * lf_ref[j : j + 1, lanes(l)]
                window = xs[l, pl.ds(PAD + r0 - j, 64), :]
                both = jnp.where(near >= j, window, 0.0) * here
                out.append(sums[j] + jnp.sum(both.reshape(8, 8, 128), axis=0))
            grad = gg_ref[pl.ds(pl.multiple_of(r0, 16), 64), lanes(l)].astype(F32)
            gf[0, l, rows_at(r0, 64), :] = grad * filt[l, rows_at(r0, 64), :]
            gf[1, l, rows_at(r0, 64), :] = total * feats[2, l, rows_at(r0, 64), :]
            gf[2, l, rows_at(r0, 64), :] = total * feats[1, l, rows_at(r0, 64), :]
            return tuple(out)

        sums = lax.fori_loop(0, 4, step, (jnp.zeros((8, 128), F32),) * BLK)
        for j in range(BLK):
            near_taps[j : j + 1, lanes(l)] = jnp.sum(sums[j], axis=0, keepdims=True)
        return carry

    lax.fori_loop(0, LB, lane, 0)


def short_sums(gf, pj, age_ref, short):
    def lane(l, carry):
        def step(i, sums):
            r0 = i * 64
            age = age_ref[rows_at(128 + r0, 64), :]
            out = []
            for b in range(3):
                here = gf[b, l, rows_at(r0, 64), :]
                for tap in range(3):
                    window = pj[b, l, pl.ds(PAD + r0 - tap, 64), :]
                    if tap:
                        window = jnp.where(age >= tap, window, 0.0)
                    out.append(sums[b * 3 + tap] + jnp.sum((here * window).reshape(8, 8, 128), axis=0))
            return tuple(out)

        sums = lax.fori_loop(0, 4, step, (jnp.zeros((8, 128), F32),) * 9)
        for at in range(9):
            short[at : at + 1, lanes(l)] = jnp.sum(sums[at], axis=0, keepdims=True)
        return carry

    lax.fori_loop(0, LB, lane, 0)


def input_grads(gf, fw_ref, room_ref, gproj_ref):
    def step(at, carry):
        l, r0 = at // 4, (at % 4) * 64
        room = room_ref[rows_at(128 + r0, 64), :]
        for b in range(3):
            total = gf[b, l, rows_at(r0, 64), :] * fw_ref[b, 0:1, lanes(l)]
            for tap in range(1, 3):
                later = gf[b, l, pl.ds(r0 + tap, 64), :]
                total = total + jnp.where(room > tap, later, 0.0) * fw_ref[b, tap : tap + 1, lanes(l)]
            gproj_ref[b, pl.ds(pl.multiple_of(r0, 16), 64), lanes(l)] = total.astype(BF16)
        return carry

    lax.fori_loop(0, LB * 4, step, 0)


MESH = pl.DeviceIdType.MESH
NX = 4
COLS = 384
WIDE = NX * COLS
OWN = 32
PEERS = 16


def turned(at, by):
    return lax.rem(at + by + 2 * NX, NX)


def kernel(
    seg_ref, proj_ref, fw_ref, lf_ref, w_ref, cot_ref, tab_ref, tabt_ref,
    out_ref, gproj_ref, taps_ref, short_ref,
    pj, feats, filt, xs, xv, prod, jhalo, phalo, age_ref, room_ref, lfb, spec_x, spec_g, spec_y, wide,
    gs_, gl, gv, glhalo, spec_z, spec_q, gf, gfhalo, taps, near_taps, short,
    wg, cg, ga_own, ga_back, ga_fore, ga_far, part_own, part_back, part_fore, part_far, rs_a, rs_b, rs_c, rs_t, gg,
    ob_own, ob_back, ob_fore, ob_far, co_own, co_back, co_fore, co_far, sb, y_a, y_b, y_c, y_t, rb, fin, pk, rk, tot, fk,
    send, recv, t_send, t_recv, u_send, u_recv,
):
    ctx, tp = lax.axis_index("ctx"), lax.axis_index("tp")
    z, x, y, core = ctx // 4, ctx % 4, tp // 2, tp % 2
    way = 1 - 2 * core
    other = (ctx, y * 2 + (1 - core))

    def at_x(by):
        return (z * 4 + turned(x, by), tp)

    def at_z(by):
        return (turned(z, by) * 4 + x, tp)

    def at_y(by):
        return (ctx, turned(y, by) * 2 + core)

    def at_ctx(by):
        return (lax.rem(ctx + by + PEERS, PEERS), tp)

    barrier = pltpu.get_barrier_semaphore()
    for by in range(1, PEERS):
        pl.semaphore_signal(barrier, inc=1, device_id=at_ctx(by), device_id_type=MESH)
    for peer in (at_y(1), at_y(-1), other):
        pl.semaphore_signal(barrier, inc=1, device_id=peer, device_id_type=MESH)
    pl.semaphore_wait(barrier, PEERS + 2)

    started = []

    def remote(slot, source, target, peer):
        copy = pltpu.make_async_remote_copy(
            src_ref=source, dst_ref=target, send_sem=send.at[slot], recv_sem=recv.at[slot],
            device_id=peer, device_id_type=MESH,
        )
        copy.start()
        started.append(copy)
        return copy

    w_ahead = remote(0, w_ref, wg.at[x], at_x(way))
    w_behind = remote(1, w_ref, wg.at[x], at_x(-way))
    cot_in = []
    for by in range(1, 4):
        cols = pl.ds(pl.multiple_of(turned(z, by) * WIDE, 128), WIDE)
        cot_in.append(remote(2 + by, cot_ref.at[:, cols], cg.at[tp, z], at_z(by)))
    j_copy = remote(13, proj_ref.at[:, pl.ds(ROWS - 16, 16), :], jhalo, at_ctx(1))
    wg[x] = w_ref[...]
    cg[tp, z] = cot_ref[:, pl.ds(pl.multiple_of(z * WIDE, 128), WIDE)]

    find_ages(seg_ref, ctx * ROWS, age_ref, room_ref)
    load_inputs(proj_ref, pj, PAD, ROWS)
    xs[:, 0:PAD, :] = jnp.zeros((LB, PAD, 128), F32)
    features(pj, fw_ref, age_ref, room_ref, feats, xs, xv, prod, 2, 2)
    p_copy = remote(14, prod, phalo, at_ctx(1))

    def slab(by):
        return cg.at[turned(y, by) * 2 + core]

    for copy in cot_in:
        copy.wait_recv()
    cot_ahead = remote(6, slab(0), slab(0), at_y(way))
    cot_behind = remote(7, slab(0), slab(0), at_y(-way))
    cot_core = [remote(9, slab(0), slab(0), other)]

    j_copy.wait_recv()
    load_inputs(jhalo, pj, 0, PAD)
    features(pj, fw_ref, age_ref, room_ref, feats, xs, xv, prod, 0, 2)
    lfb[...] = lf_ref[...].astype(BF16)
    transform(tab_ref[2], lfb, spec_g, 0)
    for group in (1, 2):
        transform(tab_ref[0], xv, spec_x, group)

    p_copy.wait_recv()
    mask_halo(phalo, room_ref, xv)
    transform(tab_ref[0], xv, spec_x, 0)
    cot_ahead.wait_recv()
    cot_on = remote(8, slab(-way), slab(-way), at_y(way))
    cot_core.append(remote(10, slab(-way), slab(-way), other))
    cot_behind.wait_recv()
    cot_core.append(remote(11, slab(way), slab(way), other))
    far_forward(spec_x, spec_g, age_ref, spec_y)
    inverse(tabt_ref[1], spec_y, wide, 2)
    w_ahead.wait_recv()
    w_on = remote(2, wg.at[turned(x, -way)], wg.at[turned(x, -way)], at_x(way))
    near_forward(xs, lf_ref, age_ref, wide, feats, filt, ga_own)
    ga_ahead = remote(15, ga_own, ga_back, at_z(way))
    ga_behind = remote(16, ga_own, ga_fore, at_z(-way))

    cot_on.wait_recv()
    cot_core.append(remote(12, slab(2), slab(2), other))
    for copy in cot_core:
        copy.wait_recv()
    w_behind.wait_recv()
    w_on.wait_recv()

    def backward_part(block, target):
        def step(n, carry):
            rows = pl.ds(pl.multiple_of(n * 256, 256), 256)
            total = jnp.zeros((ROWS, 256), F32)
            for at in range(NX):
                total = total + lax.dot_general(
                    cg[:, block, :, at * COLS : (at + 1) * COLS].reshape(ROWS, COLS), wg[at, rows, :],
                    (((1,), (1,)), ((), ())), preferred_element_type=F32,
                )
            target[:, rows] = total.astype(BF16)
            return carry

        lax.fori_loop(0, CH // 256, step, 0)

    backward_part(turned(z, 2), part_far)
    s_a = remote(18, part_far, rs_a, at_z(way))
    backward_part(turned(z, -way), part_back)
    s_b = remote(19, part_back, rs_b, at_z(-way))
    ga_ahead.wait_recv()
    ga_on = remote(17, ga_back, ga_far, at_z(way))
    backward_part(turned(z, way), part_fore)
    backward_part(z, part_own)

    def forward_part(rows, target):
        def step(at, carry):
            got = jnp.dot(rows[...], wg[at], preferred_element_type=F32)
            cols = pl.ds(pl.multiple_of(at * COLS, 128), COLS)
            target[:, :, :, cols] = got.astype(BF16).reshape(4, 2, OWN, COLS)
            return carry

        lax.fori_loop(0, NX, step, 0)

    forward_part(ga_own, ob_own)
    o_core = [remote(21, ob_own.at[:, 1 - core], co_own, other)]

    s_a.wait_recv()

    def add_rows(target, terms, count):
        def step(i, carry):
            rows = pl.ds(pl.multiple_of(i * 64, 64), 64)
            total = terms[0][rows, :].astype(F32)
            for term in terms[1:]:
                total = total + term[rows, :].astype(F32)
            target[rows, :] = total.astype(BF16)
            return carry

        lax.fori_loop(0, count // 64, step, 0)

    add_rows(rs_t, (rs_a, part_fore), ROWS)
    s_c = remote(20, rs_t, rs_c, at_z(way))

    forward_part(ga_back, ob_back)
    o_core.append(remote(22, ob_back.at[:, 1 - core], co_fore, other))
    ga_behind.wait_recv()
    forward_part(ga_fore, ob_fore)
    o_core.append(remote(23, ob_fore.at[:, 1 - core], co_back, other))
    ga_on.wait_recv()
    forward_part(ga_far, ob_far)
    o_core.append(remote(24, ob_far.at[:, 1 - core], co_far, other))

    s_b.wait_recv()
    s_c.wait_recv()
    add_rows(gg, (part_own, rs_b, rs_c), ROWS)
    make_long(gg, feats, age_ref, gs_, gl, gv, 0, 2)
    l_copy = remote(31, gl, glhalo, at_ctx(-1))

    for copy in o_core:
        copy.wait_recv()

    def add_core(q, carry):
        blocks = ((0, ob_own, co_own), (-way, ob_back, co_back), (way, ob_fore, co_fore), (2, ob_far, co_far))
        for by, mine, theirs in blocks:
            sb[q, turned(z, by)] = (mine[q, core].astype(F32) + theirs[q].astype(F32)).astype(BF16)
        return carry

    lax.fori_loop(0, 4, add_core, 0)
    y_1 = remote(25, sb.at[turned(y, 2)], y_a, at_y(way))
    y_2 = remote(26, sb.at[turned(y, -way)], y_b, at_y(-way))

    make_long(gg, feats, age_ref, gs_, gl, gv, 2, 2)
    gs_[:, ROWS : ROWS + PAD, :] = jnp.zeros((LB, PAD, 128), F32)
    for group in (0, 1):
        transform(tab_ref[1], gv, spec_z, group)
    far_taps(spec_x, spec_z, age_ref, spec_q)

    y_1.wait_recv()

    def add_blocks(target, terms):
        for zz in range(4):
            total = terms[0][zz].astype(F32)
            for term in terms[1:]:
                total = total + term[zz].astype(F32)
            target[zz] = total.astype(BF16)

    add_blocks(y_t, (y_a, sb.at[turned(y, way)]))
    y_3 = remote(27, y_t, y_c, at_y(way))

    l_copy.wait_recv()
    mask_next(glhalo, age_ref, gv)
    transform(tab_ref[1], gv, spec_z, 2)
    far_back(spec_z, spec_g, age_ref, spec_y)
    inverse(tabt_ref[0], spec_y, wide, 2)
    near_back(gs_, xs, lf_ref, age_ref, room_ref, wide, gg, filt, feats, gf, near_taps)
    f_copy = remote(32, gf.at[:, :, pl.ds(0, 8), :], gfhalo, at_ctx(-1))

    y_2.wait_recv()
    y_3.wait_recv()
    add_blocks(rb, (sb.at[y], y_b, y_c))
    outs = [remote(27 + by, rb.at[turned(z, by)], fin.at[z], at_z(by)) for by in range(1, 4)]

    inverse(tabt_ref[2], spec_q, taps, 1)
    taps[0:BLK, :] = taps[0:BLK, :] + near_taps[...]
    short_sums(gf, pj, age_ref, short)
    for q in range(PEERS):
        rows = taps[q * 8 : (q + 1) * 8, :]
        pk[q, :, 0:512] = jnp.concatenate([rows[:, 0:512], rows[:, 512:1024]], axis=0).astype(BF16)
        if q < 9:
            row = [short[q : q + 1, i * 128 : (i + 1) * 128] for i in range(8)]
            row.append(jnp.zeros((8, 128), F32))
            pk[q, :, 512:640] = jnp.concatenate(row, axis=0).astype(BF16)
        else:
            pk[q, :, 512:640] = jnp.zeros((16, 128), BF16)

    def tap_copy(i):
        peer = lax.rem(ctx + i, PEERS)
        return pltpu.make_async_remote_copy(
            src_ref=pk.at[peer], dst_ref=rk.at[i], send_sem=t_send.at[i], recv_sem=t_recv.at[i],
            device_id=(peer, tp), device_id_type=MESH,
        )

    def total_copy(i):
        peer = lax.rem(ctx + i, PEERS)
        return pltpu.make_async_remote_copy(
            src_ref=tot, dst_ref=fk.at[ctx], send_sem=u_send.at[i], recv_sem=u_recv.at[i],
            device_id=(peer, tp), device_id_type=MESH,
        )

    def each(make, act):
        def step(i, carry):
            act(make(i))
            return carry

        lax.fori_loop(1, PEERS, step, 0)

    each(tap_copy, lambda copy: copy.start())
    f_copy.wait_recv()
    gf[:, :, ROWS : ROWS + 8, :] = gfhalo[...]
    input_grads(gf, fw_ref, room_ref, gproj_ref)

    for copy in outs:
        copy.wait_recv()
    out_ref[:, pl.ds(pl.multiple_of(z * WIDE, 128), WIDE)] = rb[z]
    for by in range(1, 4):
        block = turned(z, by)
        out_ref[:, pl.ds(pl.multiple_of(block * WIDE, 128), WIDE)] = fin[block]

    each(tap_copy, lambda copy: copy.wait_recv())
    total = pk[ctx].astype(F32)
    for i in range(1, PEERS):
        total = total + rk[i].astype(F32)
    tot[...] = total.astype(BF16)
    fk[ctx] = tot[...]
    each(total_copy, lambda copy: copy.start())
    each(total_copy, lambda copy: copy.wait_recv())
    norm = TOKENS**-0.5
    for q in range(PEERS):
        done = fk[q].astype(F32) * norm
        taps_ref[q * 8 : (q + 1) * 8, 0:512] = done[0:8, 0:512]
        taps_ref[q * 8 : (q + 1) * 8, 512:1024] = done[8:16, 0:512]
        if q < 9:
            for i in range(8):
                short_ref[q // 3, q % 3 : q % 3 + 1, i * 128 : (i + 1) * 128] = done[i : i + 1, 512:640]

    each(tap_copy, lambda copy: copy.wait_send())
    each(total_copy, lambda copy: copy.wait_send())
    for copy in started:
        copy.wait_send()


def shards(projected, feat_weight, long_filter, out_weight, seg_lengths, cotangent):
    tab, tabt = (jnp.asarray(t) for t in tables())
    vm = pl.BlockSpec(memory_space=pltpu.VMEM)
    laned = (LB, ROWS, 128)
    padded = (LB, PAD + ROWS, 128)
    spec = (3 * 256, CH)
    age = (512, 128)
    block = (4, OWN, WIDE)
    scratch = [
        ((3,) + padded, F32), ((3,) + laned, F32), (laned, F32), (padded, F32), ((128 + ROWS, CH), BF16),
        ((128, CH), BF16), ((3, 16, CH), BF16), ((128, CH), BF16), (age, jnp.int32), (age, jnp.int32),
        ((128, CH), BF16), (spec, F32), ((256, CH), F32), ((512, CH), F32), ((ROWS, CH), F32),
        (padded, F32), ((128, CH), BF16), ((ROWS + 128, CH), BF16), ((128, CH), BF16), (spec, F32), ((256, CH), F32),
        ((3,) + padded, F32), ((3, LB, 8, 128), F32), ((128, CH), F32), ((BLK, CH), F32), ((16, CH), F32),
        ((NX, CH, COLS), BF16), ((8,) + block, BF16),
        *[((ROWS, CH), BF16)] * 13, *[((4, 2, OWN, WIDE), BF16)] * 4, *[(block, BF16)] * 4, ((4,) + block, BF16),
        (block, BF16), (block, BF16), (block, BF16), (block, BF16), (block, BF16), (block, BF16),
        ((PEERS, 16, 640), BF16), ((PEERS, 16, 640), BF16), ((16, 640), BF16), ((PEERS, 16, 640), BF16),
    ]
    dma = pltpu.SemaphoreType.DMA
    return pl.pallas_call(
        kernel,
        out_shape=[
            jax.ShapeDtypeStruct((OWN, 4 * WIDE), BF16),
            jax.ShapeDtypeStruct((3, ROWS, CH), BF16),
            jax.ShapeDtypeStruct((128, CH), F32),
            jax.ShapeDtypeStruct((3, 3, CH), F32),
        ],
        in_specs=[pl.BlockSpec(memory_space=pltpu.SMEM)] + [vm] * 7,
        out_specs=[vm] * 4,
        scratch_shapes=[pltpu.VMEM(s, d) for s, d in scratch]
        + [dma((33,)), dma((33,)), dma((PEERS,)), dma((PEERS,)), dma((PEERS,)), dma((PEERS,))],
        compiler_params=pltpu.CompilerParams(
            collective_id=0, has_side_effects=True, vmem_limit_bytes=60 * 2**20
        ),
    )(seg_lengths, projected, feat_weight, long_filter, out_weight, cotangent, tab, tabt)


def solution(mesh):
    return jax.shard_map(
        shards,
        mesh=mesh,
        in_specs=(
            P(None, "ctx", "tp"),
            P(None, None, "tp"),
            P(None, "tp"),
            P("tp", "ctx"),
            P(),
            P(("ctx", "tp"), None),
        ),
        out_specs=(
            P(("ctx", "tp"), None),
            P(None, "ctx", "tp"),
            P(None, "tp"),
            P(None, None, "tp"),
        ),
        check_vma=False,
    )
```

```python
import jax
import jax.numpy as jnp
import numpy as np
from jax import lax
from jax.experimental import pallas as pl
from jax.experimental.pallas import tpu as pltpu
from jax.sharding import PartitionSpec as P

F32 = jnp.float32
BF16 = jnp.bfloat16
ROWS = 256
CH = 1024
LB = CH // 128
BLK = 16
FAR = 8
TOKENS = 4096
NSEG = 32
PAD = 16
CHUNKS = 4
SPAN = LB // CHUNKS


def tables():
    turn = np.pi * (2 * np.arange(BLK) + 1) / (2 * BLK)

    def wave(at):
        return np.concatenate([np.cos(np.outer(turn, at)), -np.sin(np.outer(turn, at))])

    into = wave(np.arange(BLK))
    back = wave(np.arange(BLK) + BLK) / BLK
    back[BLK:] = -back[BLK:]
    taps = np.zeros((FAR * 2 * BLK, FAR * BLK))
    window = wave(np.arange(2 * BLK))
    for k in range(FAR):
        for d in range(1, 2 * BLK):
            if k * BLK + d < FAR * BLK:
                taps[k * 2 * BLK : (k + 1) * 2 * BLK, k * BLK + d] = window[:, d]
    each = np.eye(FAR)
    stack = np.stack([np.kron(each, into), np.kron(each, back), taps])
    return stack.astype(jnp.bfloat16), np.swapaxes(stack, 1, 2).astype(jnp.bfloat16)


def lanes(l):
    return pl.ds(pl.multiple_of(l * 128, 128), 128)


def rows_at(start, count):
    return pl.ds(pl.multiple_of(start, 8), count)


def find_ages(seg_ref, base, age_ref, room_ref):
    def chunk(i, carry):
        at = rows_at(i * 64, 64)
        pos = lax.broadcasted_iota(jnp.int32, (64, 128), 0) + (base - 128 + i * 64)

        def one(k, state):
            start, latest, after = state
            end = start + seg_ref[k]
            inside = pos >= start
            return end, jnp.where(inside, start, latest), jnp.where(inside, end, after)

        zero = jnp.zeros((64, 128), jnp.int32)
        _, latest, after = lax.fori_loop(0, NSEG, one, (jnp.int32(0), zero, zero))
        age_ref[at, :] = jnp.where(pos < TOKENS, pos - latest, -1)
        room_ref[at, :] = after - pos
        return carry

    lax.fori_loop(0, 8, chunk, 0)


def in_block(count):
    return lax.rem(lax.broadcasted_iota(jnp.int32, (count, 128), 0), BLK)


def load_inputs(source, pj, first, count):
    def lane(l, carry):
        for b in range(3):
            pj[b, l, first : first + count, :] = source[b, :, lanes(l)].astype(F32)
        return carry

    lax.fori_loop(0, LB, lane, 0)


def features(pj, fw_ref, age_ref, room_ref, feats, xs, xv, prod, first, count):
    def step(at, carry):
        l, r0 = at // count, (first + at % count) * 64
        age = age_ref[rows_at(128 + r0, 64), :]
        inside = in_block(64)
        got = []
        for b in range(3):
            total = pj[b, l, rows_at(PAD + r0, 64), :] * fw_ref[b, 0:1, lanes(l)]
            for i in range(1, 3):
                window = pj[b, l, pl.ds(PAD + r0 - i, 64), :]
                total = total + jnp.where(age >= i, window, 0.0) * fw_ref[b, i : i + 1, lanes(l)]
            feats[b, l, rows_at(r0, 64), :] = total
            got.append(total)
        product = (got[1] * got[2]).astype(BF16)
        wide = product.astype(F32)
        xs[l, rows_at(PAD + r0, 64), :] = wide
        live = room_ref[rows_at(128 + r0, 64), :] >= BLK - inside
        xv[pl.ds(pl.multiple_of(128 + r0, 16), 64), lanes(l)] = jnp.where(live, wide, 0.0).astype(BF16)
        if first:
            prod[pl.ds(pl.multiple_of(r0 - 128, 16), 64), lanes(l)] = product
        return carry

    lax.fori_loop(0, LB * count, step, 0)


def mask_halo(phalo_ref, room_ref, xv):
    def step(at, carry):
        l, r0 = at // 2, (at % 2) * 64
        live = room_ref[rows_at(r0, 64), :] >= BLK - in_block(64)
        rows = pl.ds(pl.multiple_of(r0, 16), 64)
        xv[rows, lanes(l)] = jnp.where(live, phalo_ref[rows, lanes(l)].astype(F32), 0.0).astype(BF16)
        return carry

    lax.fori_loop(0, LB * 2, step, 0)


def chunk_cols(c):
    return pl.ds(pl.multiple_of(c * 256, 256), 256)


def transform(table, source, target, group, c):
    target[group * 256 : (group + 1) * 256, chunk_cols(c)] = jnp.dot(
        table, source[group * 128 : (group + 1) * 128, chunk_cols(c)], preferred_element_type=F32
    )


def all_chunks(act):
    def step(c, carry):
        act(c)
        return carry

    lax.fori_loop(0, CHUNKS, step, 0)


GROUP = 16


def pair(ref, at, l, ft):
    base = at * 32 + ft * 8
    return ref[rows_at(base, 8), lanes(l)], ref[rows_at(base + 16, 8), lanes(l)]


def reach_of(age_ref, m):
    return jnp.broadcast_to(age_ref[pl.ds(128 + m * BLK - 1, 1), :], (8, 128))


def where_pair(live, value):
    return jnp.where(live, value[0], 0.0), jnp.where(live, value[1], 0.0)


def times(a, b):
    return a[0] * b[0] - a[1] * b[1], a[0] * b[1] + a[1] * b[0]


def far_forward(spec_x, spec_g, age_ref, spec_y):
    def outer(at, carry):
        l, ft = at // 2, at % 2
        g = [pair(spec_g, k, l, ft) for k in range(FAR)]

        def inner(q, carry):
            m0 = q * GROUP
            x = [pair(spec_x, m0 + i, l, ft) for i in range(FAR + GROUP - 1)]
            for m in range(GROUP):
                reach = reach_of(age_ref, m0 + m)
                terms = []
                for k in range(1, FAR + 1):
                    terms.append(times(g[k - 1], where_pair(reach >= BLK * (k - 1), x[FAR + m - k])))
                re = sum(t[0] for t in terms[1:]) + terms[0][0]
                im = sum(t[1] for t in terms[1:]) + terms[0][1]
                spec_y[rows_at((m0 + m) * 32 + ft * 8, 8), lanes(l)] = re
                spec_y[rows_at((m0 + m) * 32 + 16 + ft * 8, 8), lanes(l)] = -im
            return carry

        lax.fori_loop(0, ROWS // BLK // GROUP, inner, 0)
        return carry

    lax.fori_loop(0, LB * 2, outer, 0)


def far_back(spec_z, spec_g, age_ref, spec_p, c):
    def outer(at, carry):
        l, ft = c * SPAN + at // 2, at % 2
        g = [pair(spec_g, k, l, ft) for k in range(FAR)]

        def inner(q, carry):
            n0 = q * GROUP
            z = [pair(spec_z, n0 + 1 + i, l, ft) for i in range(FAR + GROUP - 1)]
            reach = [reach_of(age_ref, n0 + 1 + i) for i in range(FAR + GROUP - 1)]
            for n in range(GROUP):
                terms = []
                for k in range(1, FAR + 1):
                    terms.append(times(g[k - 1], where_pair(reach[n + k - 1] >= BLK * (k - 1), z[n + k - 1])))
                re = sum(t[0] for t in terms[1:]) + terms[0][0]
                im = sum(t[1] for t in terms[1:]) + terms[0][1]
                spec_p[rows_at((n0 + n) * 32 + ft * 8, 8), lanes(l)] = re
                spec_p[rows_at((n0 + n) * 32 + 16 + ft * 8, 8), lanes(l)] = -im
            return carry

        lax.fori_loop(0, ROWS // BLK // GROUP, inner, 0)
        return carry

    lax.fori_loop(0, SPAN * 2, outer, 0)


def far_taps(spec_x, spec_z, age_ref, spec_q, c):
    def outer(at, carry):
        l, ft = c * SPAN + at // 2, at % 2

        def inner(q, state):
            m0 = q * GROUP
            x = [pair(spec_x, m0 + i, l, ft) for i in range(FAR + GROUP - 1)]
            for m in range(GROUP):
                reach = reach_of(age_ref, m0 + m)
                z = pair(spec_z, m0 + m, l, ft)
                out = []
                for k in range(1, FAR + 1):
                    re, im = times(where_pair(reach >= BLK * (k - 1), x[FAR + m - k]), z)
                    out += [state[2 * k - 2] + re, state[2 * k - 1] + im]
                state = tuple(out)
            return state

        zero = jnp.zeros((8, 128), F32)
        state = lax.fori_loop(0, ROWS // BLK // GROUP, inner, (zero,) * (2 * FAR))
        for k in range(FAR):
            spec_q[rows_at(k * 32 + ft * 8, 8), lanes(l)] = state[2 * k]
            spec_q[rows_at(k * 32 + 16 + ft * 8, 8), lanes(l)] = -state[2 * k + 1]
        return carry

    lax.fori_loop(0, SPAN * 2, outer, 0)


def inverse(table, source, target, groups, c):
    for group in range(groups):
        target[group * 128 : (group + 1) * 128, chunk_cols(c)] = jnp.dot(
            table, source[group * 256 : (group + 1) * 256, chunk_cols(c)].astype(BF16), preferred_element_type=F32
        )


def near_forward(xs, lf_ref, age_ref, wide, feats, filt, gated):
    def step(at, carry):
        l, r0 = at // 4, (at % 4) * 64
        age = age_ref[rows_at(128 + r0, 64), :]
        inside = in_block(64)
        near = jnp.minimum(age, inside)
        total = jnp.where(age > inside, wide[rows_at(r0, 64), lanes(l)], 0.0)
        for j in range(BLK):
            window = xs[l, pl.ds(PAD + r0 - j, 64), :]
            total = total + jnp.where(near >= j, window, 0.0) * lf_ref[j : j + 1, lanes(l)]
        filt[l, rows_at(r0, 64), :] = total
        gate = feats[0, l, rows_at(r0, 64), :] * total
        gated[pl.ds(pl.multiple_of(r0, 16), 64), lanes(l)] = gate.astype(BF16)
        return carry

    lax.fori_loop(0, LB * 4, step, 0)


def make_long(gg_ref, feats, age_ref, gs_, gl, gv, c):
    def step(at, carry):
        lane, r0 = at // 4, (at % 4) * 64
        l = c * SPAN + lane
        rows = pl.ds(pl.multiple_of(r0, 16), 64)
        sent = (gg_ref[rows, lanes(l)].astype(F32) * feats[0, l, rows_at(r0, 64), :]).astype(BF16)
        long = sent.astype(F32)
        gl[rows, lanes(lane)] = sent
        gs_[l, rows_at(r0, 64), :] = long
        live = age_ref[rows_at(128 + r0, 64), :] > in_block(64)
        gv[rows, lanes(l)] = jnp.where(live, long, 0.0).astype(BF16)
        return carry

    lax.fori_loop(0, SPAN * 4, step, 0)


def mask_next(glhalo_ref, age_ref, gv, c):
    def step(at, carry):
        lane, r0 = at // 2, (at % 2) * 64
        live = age_ref[rows_at(128 + ROWS + r0, 64), :] > in_block(64)
        long = glhalo_ref[pl.ds(pl.multiple_of(r0, 16), 64), lanes(lane)].astype(F32)
        rows = pl.ds(pl.multiple_of(ROWS + r0, 16), 64)
        gv[rows, lanes(c * SPAN + lane)] = jnp.where(live, long, 0.0).astype(BF16)
        return carry

    lax.fori_loop(0, SPAN * 2, step, 0)


def near_back(gs_, xs, lf_ref, age_ref, room_ref, wide, gg_ref, filt, feats, gf, near_taps, c):
    def lane(at, carry):
        l = c * SPAN + at

        def step(i, sums):
            r0 = i * 64
            age = age_ref[rows_at(128 + r0, 64), :]
            room = room_ref[rows_at(128 + r0, 64), :]
            inside = in_block(64)
            near = jnp.minimum(age, inside)
            ahead = jnp.minimum(room, BLK - inside)
            here = gs_[l, rows_at(r0, 64), :]
            total = jnp.where(room >= BLK - inside, wide[rows_at(r0, 64), lanes(l)], 0.0)
            out = []
            for j in range(BLK):
                later = gs_[l, pl.ds(r0 + j, 64), :]
                total = total + jnp.where(ahead > j, later, 0.0) * lf_ref[j : j + 1, lanes(l)]
                window = xs[l, pl.ds(PAD + r0 - j, 64), :]
                both = jnp.where(near >= j, window, 0.0) * here
                out.append(sums[j] + jnp.sum(both.reshape(8, 8, 128), axis=0))
            grad = gg_ref[pl.ds(pl.multiple_of(r0, 16), 64), lanes(l)].astype(F32)
            gf[0, l, rows_at(r0, 64), :] = grad * filt[l, rows_at(r0, 64), :]
            gf[1, l, rows_at(r0, 64), :] = total * feats[2, l, rows_at(r0, 64), :]
            gf[2, l, rows_at(r0, 64), :] = total * feats[1, l, rows_at(r0, 64), :]
            return tuple(out)

        sums = lax.fori_loop(0, 4, step, (jnp.zeros((8, 128), F32),) * BLK)
        for j in range(BLK):
            near_taps[j : j + 1, lanes(l)] = jnp.sum(sums[j], axis=0, keepdims=True)
        return carry

    lax.fori_loop(0, SPAN, lane, 0)


def short_sums(gf, pj, age_ref, short):
    def lane(l, carry):
        def step(i, sums):
            r0 = i * 64
            age = age_ref[rows_at(128 + r0, 64), :]
            out = []
            for b in range(3):
                here = gf[b, l, rows_at(r0, 64), :]
                for tap in range(3):
                    window = pj[b, l, pl.ds(PAD + r0 - tap, 64), :]
                    if tap:
                        window = jnp.where(age >= tap, window, 0.0)
                    out.append(sums[b * 3 + tap] + jnp.sum((here * window).reshape(8, 8, 128), axis=0))
            return tuple(out)

        sums = lax.fori_loop(0, 4, step, (jnp.zeros((8, 128), F32),) * 9)
        for at in range(9):
            short[at : at + 1, lanes(l)] = jnp.sum(sums[at], axis=0, keepdims=True)
        return carry

    lax.fori_loop(0, LB, lane, 0)


def input_grads(gf, fw_ref, room_ref, gproj_ref):
    def step(at, carry):
        l, r0 = at // 4, (at % 4) * 64
        room = room_ref[rows_at(128 + r0, 64), :]
        for b in range(3):
            total = gf[b, l, rows_at(r0, 64), :] * fw_ref[b, 0:1, lanes(l)]
            for tap in range(1, 3):
                later = gf[b, l, pl.ds(r0 + tap, 64), :]
                total = total + jnp.where(room > tap, later, 0.0) * fw_ref[b, tap : tap + 1, lanes(l)]
            gproj_ref[b, pl.ds(pl.multiple_of(r0, 16), 64), lanes(l)] = total.astype(BF16)
        return carry

    lax.fori_loop(0, LB * 4, step, 0)


MESH = pl.DeviceIdType.MESH
NX = 4
COLS = 384
WIDE = NX * COLS
OWN = 32
PEERS = 16


def turned(at, by):
    return lax.rem(at + by + 2 * NX, NX)


class Bag:
    pass


LANED = (LB, ROWS, 128)
PADDED = (LB, PAD + ROWS, 128)
SPEC = (3 * 256, CH)
AGE = (512, 128)
PART = (ROWS, CH // CHUNKS)
BLOCK = (OWN, WIDE)
ROLES = ("own", "back", "fore", "far")
PLACES = dict(
    pj=((3,) + PADDED, F32), feats=((3,) + LANED, F32), filt=(LANED, F32), xs=(PADDED, F32),
    xv=((128 + ROWS, CH), BF16), prod=((128, CH), BF16), jhalo=((3, 16, CH), BF16), phalo=((128, CH), BF16),
    age=(AGE, jnp.int32), room=(AGE, jnp.int32), lfb=((128, CH), BF16), spec_x=(SPEC, F32),
    spec_g=((256, CH), F32), spec_y=((512, CH), F32), wide=((ROWS, CH), F32), gs=(PADDED, F32),
    gv=((ROWS + 128, CH), BF16), spec_z=(SPEC, F32), spec_q=((256, CH), F32), gf=((3,) + PADDED, F32),
    gfhalo=((3, LB, 8, 128), F32), taps=((128, CH), F32), near_taps=((BLK, CH), F32), short=((16, CH), F32),
    cg=((8, 4) + BLOCK, BF16), gg=((ROWS, CH), BF16),
    pk=((PEERS, 16, 640), BF16), rk=((PEERS, 16, 640), BF16), tot=((16, 640), BF16), fk=((PEERS, 16, 640), BF16),
)
for _c in range(CHUNKS):
    PLACES["wg%d" % _c] = ((NX, CH // CHUNKS, COLS), BF16)
    PLACES["gl%d" % _c] = (PART, BF16)
    PLACES["glhalo%d" % _c] = ((128, CH // CHUNKS), BF16)
    for _r in ROLES:
        PLACES["part_%s%d" % (_r, _c)] = (PART, BF16)
    for _r in "abct":
        PLACES["rs_%s%d" % (_r, _c)] = (PART, BF16)
for _r in ROLES:
    PLACES["ga_" + _r] = ((ROWS, CH), BF16)
    PLACES["ob_" + _r] = ((4, 2) + BLOCK, BF16)
    PLACES["co_" + _r] = ((4,) + BLOCK, BF16)
    PLACES["sb_" + _r] = ((4,) + BLOCK, BF16)
    for _k in "abct":
        PLACES["y%s_%s" % (_k, _r)] = (BLOCK, BF16)
    PLACES["rb_" + _r] = (BLOCK, BF16)
    PLACES["fin_" + _r] = (BLOCK, BF16)
SLOTS = 96


def kernel(
    seg_ref, proj_ref, fw_ref, lf_ref, w_ref, cot_ref, tab_ref, tabt_ref,
    out_ref, gproj_ref, taps_ref, short_ref, *scratch,
):
    s = Bag()
    for name, ref in zip(PLACES, scratch):
        setattr(s, name, ref)
    send, recv, t_send, t_recv, u_send, u_recv = scratch[len(PLACES) :]

    def of(name, which):
        return getattr(s, name + str(which))

    ctx, tp = lax.axis_index("ctx"), lax.axis_index("tp")
    z, x, y, core = ctx // 4, ctx % 4, tp // 2, tp % 2
    way = 1 - 2 * core
    other = (ctx, y * 2 + (1 - core))

    def at_x(by):
        return (z * 4 + turned(x, by), tp)

    def at_z(by):
        return (turned(z, by) * 4 + x, tp)

    def at_y(by):
        return (ctx, turned(y, by) * 2 + core)

    def at_ctx(by):
        return (lax.rem(ctx + by + PEERS, PEERS), tp)

    barrier = pltpu.get_barrier_semaphore()
    for by in range(1, PEERS):
        pl.semaphore_signal(barrier, inc=1, device_id=at_ctx(by), device_id_type=MESH)
    for peer in (at_y(1), at_y(-1), other):
        pl.semaphore_signal(barrier, inc=1, device_id=peer, device_id_type=MESH)
    pl.semaphore_wait(barrier, PEERS + 2)

    started = []

    def remote(source, target, peer):
        slot = len(started)
        copy = pltpu.make_async_remote_copy(
            src_ref=source, dst_ref=target, send_sem=send.at[slot], recv_sem=recv.at[slot],
            device_id=peer, device_id_type=MESH,
        )
        copy.start()
        started.append(copy)
        return copy

    def z_cols(by):
        return pl.ds(pl.multiple_of(turned(z, by) * WIDE, 128), WIDE)

    def slab(by):
        return cg.at[turned(y, by) * 2 + core]

    def rest(by):
        return cg.at[turned(y, by) * 2 + core, pl.ds(1, 3)]

    cg = s.cg
    mine = cot_ref.at[:, z_cols(0)]
    c_ahead = remote(mine, cg.at[tp, 0], at_y(way))
    c_behind = remote(mine, cg.at[tp, 0], at_y(-way))
    cot_in = [remote(cot_ref.at[:, z_cols(by)], cg.at[tp, 4 - by], at_z(by)) for by in (1, 3, 2)]
    j_copy = remote(proj_ref.at[:, pl.ds(ROWS - 16, 16), :], s.jhalo, at_ctx(1))
    w_ahead, w_behind, w_on = [], [], []
    for c in range(CHUNKS):
        rows = w_ref.at[pl.ds(c * 256, 256), :]
        w_ahead.append(remote(rows, of("wg", c).at[x], at_x(way)))
        w_behind.append(remote(rows, of("wg", c).at[x], at_x(-way)))
    core_copies = [remote(mine, cg.at[tp, 0], other)]
    for c in range(CHUNKS):
        of("wg", c)[x] = w_ref[c * 256 : (c + 1) * 256, :]
    cg[tp, 0] = cot_ref[:, z_cols(0)]

    find_ages(seg_ref, ctx * ROWS, s.age, s.room)
    load_inputs(proj_ref, s.pj, PAD, ROWS)
    s.xs[:, 0:PAD, :] = jnp.zeros((LB, PAD, 128), F32)
    features(s.pj, fw_ref, s.age, s.room, s.feats, s.xs, s.xv, s.prod, 2, 2)
    p_copy = remote(s.prod, s.phalo, at_ctx(1))

    s.lfb[...] = lf_ref[...].astype(BF16)
    all_chunks(lambda c: transform(tab_ref[2], s.lfb, s.spec_g, 0, c))
    c_ahead.wait_recv()
    c_on = remote(cg.at[turned(y, -way) * 2 + core, 0], cg.at[turned(y, -way) * 2 + core, 0], at_y(way))
    for copy in cot_in:
        copy.wait_recv()
    d_ahead = remote(rest(0), rest(0), at_y(way))
    d_behind = remote(rest(0), rest(0), at_y(-way))
    core_copies.append(remote(rest(0), rest(0), other))

    j_copy.wait_recv()
    load_inputs(s.jhalo, s.pj, 0, PAD)
    features(s.pj, fw_ref, s.age, s.room, s.feats, s.xs, s.xv, s.prod, 0, 2)
    for group in (1, 2):
        all_chunks(lambda c, group=group: transform(tab_ref[0], s.xv, s.spec_x, group, c))

    p_copy.wait_recv()
    mask_halo(s.phalo, s.room, s.xv)
    all_chunks(lambda c: transform(tab_ref[0], s.xv, s.spec_x, 0, c))
    far_forward(s.spec_x, s.spec_g, s.age, s.spec_y)
    d_ahead.wait_recv()
    d_on = remote(rest(-way), rest(-way), at_y(way))
    core_copies.append(remote(slab(-way), slab(-way), other))
    all_chunks(lambda c: inverse(tabt_ref[1], s.spec_y, s.wide, 2, c))
    near_forward(s.xs, lf_ref, s.age, s.wide, s.feats, s.filt, s.ga_own)
    ga_ahead = remote(s.ga_own, s.ga_back, at_z(way))
    ga_behind = remote(s.ga_own, s.ga_fore, at_z(-way))

    for c in range(CHUNKS):
        w_ahead[c].wait_recv()
        passed = of("wg", c).at[turned(x, -way)]
        w_on.append(remote(passed, passed, at_x(way)))
    c_behind.wait_recv()
    d_behind.wait_recv()
    core_copies.append(remote(slab(way), slab(way), other))
    c_on.wait_recv()
    d_on.wait_recv()
    core_copies.append(remote(slab(2), slab(2), other))
    for copy in core_copies:
        copy.wait_recv()

    def backward_part(c, by, target):
        block = turned(0, by)
        total = jnp.zeros(PART, F32)
        for at in range(NX):
            total = total + lax.dot_general(
                cg[:, block, :, at * COLS : (at + 1) * COLS].reshape(ROWS, COLS), of("wg", c)[at],
                (((1,), (1,)), ((), ())), preferred_element_type=F32,
            )
        target[...] = total.astype(BF16)

    def add_rows(target, terms):
        def step(i, carry):
            rows = pl.ds(pl.multiple_of(i * 64, 64), 64)
            total = terms[0][rows, :].astype(F32)
            for term in terms[1:]:
                total = total + term[rows, :].astype(F32)
            target(rows, total.astype(BF16))
            return carry

        lax.fori_loop(0, ROWS // 64, step, 0)

    s_a, s_b, s_c = [], [], []
    for c in range(CHUNKS):
        w_behind[c].wait_recv()
        w_on[c].wait_recv()
        backward_part(c, 2, of("part_far", c))
        s_a.append(remote(of("part_far", c), of("rs_a", c), at_z(way)))
        backward_part(c, -way, of("part_back", c))
        s_b.append(remote(of("part_back", c), of("rs_b", c), at_z(-way)))
        backward_part(c, way, of("part_fore", c))
        backward_part(c, 0, of("part_own", c))

    def forward_part(rows, target):
        def step(at, carry):
            got = jnp.zeros((ROWS, COLS), F32)
            for c in range(CHUNKS):
                got = got + jnp.dot(
                    rows[:, c * 256 : (c + 1) * 256], of("wg", c)[at], preferred_element_type=F32
                )
            cols = pl.ds(pl.multiple_of(at * COLS, 128), COLS)
            target[:, :, :, cols] = got.astype(BF16).reshape(4, 2, OWN, COLS)
            return carry

        lax.fori_loop(0, NX, step, 0)

    there = dict(own="own", back="fore", fore="back", far="far")
    o_core, y_copies, outs = {}, {}, []

    def forward_role(role):
        forward_part(of("ga_", role), of("ob_", role))
        o_core[role] = remote(of("ob_", role).at[:, 1 - core], of("co_", there[role]), other)

    def y_first(role):
        o_core[there[role]].wait_recv()
        ob, co, sb = of("ob_", role), of("co_", role), of("sb_", role)

        def step(q, carry):
            sb[q] = (ob[q, core].astype(F32) + co[q].astype(F32)).astype(BF16)
            return carry

        lax.fori_loop(0, 4, step, 0)
        y_copies[role] = [
            remote(sb.at[turned(y, 2)], of("ya_", role), at_y(way)),
            remote(sb.at[turned(y, -way)], of("yb_", role), at_y(-way)),
        ]

    def y_second(role):
        y_copies[role][0].wait_recv()
        held = of("yt_", role)
        held[...] = (of("ya_", role)[...].astype(F32) + of("sb_", role)[turned(y, way)].astype(F32)).astype(BF16)
        y_copies[role].append(remote(held, of("yc_", role), at_y(way)))

    def y_last(role):
        y_copies[role][1].wait_recv()
        y_copies[role][2].wait_recv()
        total = of("sb_", role)[y].astype(F32) + of("yb_", role)[...].astype(F32) + of("yc_", role)[...].astype(F32)
        of("rb_", role)[...] = total.astype(BF16)
        if role != "own":
            by = dict(back=-way, fore=way, far=2)[role]
            outs.append(remote(of("rb_", role), of("fin_", there[role]), at_z(by)))

    forward_role("own")
    for c in range(CHUNKS):
        s_a[c].wait_recv()
        held = of("rs_t", c)

        def put(rows, value, held=held):
            held[rows, :] = value

        add_rows(put, (of("rs_a", c), of("part_fore", c)))
        s_c.append(remote(held, of("rs_c", c), at_z(way)))
    ga_ahead.wait_recv()
    ga_on = remote(s.ga_back, s.ga_far, at_z(way))
    forward_role("back")
    ga_behind.wait_recv()
    forward_role("fore")
    y_first("own")

    l_copies = []
    s.gs[:, ROWS : ROWS + PAD, :] = jnp.zeros((LB, PAD, 128), F32)

    def back_first(c):
        s_b[c].wait_recv()
        s_c[c].wait_recv()

        def put(rows, value):
            s.gg[rows, c * 256 : (c + 1) * 256] = value

        add_rows(put, (of("part_own", c), of("rs_b", c), of("rs_c", c)))
        make_long(s.gg, s.feats, s.age, s.gs, of("gl", c), s.gv, c)
        l_copies.append(remote(of("gl", c).at[pl.ds(0, 128), :], of("glhalo", c), at_ctx(-1)))
        for group in (0, 1):
            transform(tab_ref[1], s.gv, s.spec_z, group, c)
        far_taps(s.spec_x, s.spec_z, s.age, s.spec_q, c)

    def back_second(c):
        l_copies[c].wait_recv()
        mask_next(of("glhalo", c), s.age, s.gv, c)
        transform(tab_ref[1], s.gv, s.spec_z, 2, c)
        far_back(s.spec_z, s.spec_g, s.age, s.spec_y, c)
        inverse(tabt_ref[0], s.spec_y, s.wide, 2, c)
        near_back(
            s.gs, s.xs, lf_ref, s.age, s.room, s.wide, s.gg, s.filt, s.feats, s.gf, s.near_taps, c
        )
        inverse(tabt_ref[2], s.spec_q, s.taps, 1, c)
        cols = pl.ds(c * 256, 256)
        s.taps[0:BLK, cols] = s.taps[0:BLK, cols] + s.near_taps[:, cols]

    back_first(0)
    y_first("back")
    y_first("fore")
    y_second("own")
    back_first(1)
    back_second(0)
    ga_on.wait_recv()
    forward_role("far")
    y_second("back")
    y_second("fore")
    back_first(2)
    y_first("far")
    y_last("own")
    back_second(1)
    y_last("back")
    y_last("fore")
    back_first(3)
    y_second("far")
    back_second(2)
    back_second(3)
    f_copy = remote(s.gf.at[:, :, pl.ds(0, 8), :], s.gfhalo, at_ctx(-1))
    y_last("far")

    short_sums(s.gf, s.pj, s.age, s.short)
    for q in range(PEERS):
        rows = s.taps[q * 8 : (q + 1) * 8, :]
        s.pk[q, :, 0:512] = jnp.concatenate([rows[:, 0:512], rows[:, 512:1024]], axis=0).astype(BF16)
        if q < 9:
            row = [s.short[q : q + 1, i * 128 : (i + 1) * 128] for i in range(8)]
            row.append(jnp.zeros((8, 128), F32))
            s.pk[q, :, 512:640] = jnp.concatenate(row, axis=0).astype(BF16)
        else:
            s.pk[q, :, 512:640] = jnp.zeros((16, 128), BF16)

    def tap_copy(i):
        peer = lax.rem(ctx + i, PEERS)
        return pltpu.make_async_remote_copy(
            src_ref=s.pk.at[peer], dst_ref=s.rk.at[i], send_sem=t_send.at[i], recv_sem=t_recv.at[i],
            device_id=(peer, tp), device_id_type=MESH,
        )

    def total_copy(i):
        peer = lax.rem(ctx + i, PEERS)
        return pltpu.make_async_remote_copy(
            src_ref=s.tot, dst_ref=s.fk.at[ctx], send_sem=u_send.at[i], recv_sem=u_recv.at[i],
            device_id=(peer, tp), device_id_type=MESH,
        )

    def each(make, act):
        def step(i, carry):
            act(make(i))
            return carry

        lax.fori_loop(1, PEERS, step, 0)

    each(tap_copy, lambda copy: copy.start())
    f_copy.wait_recv()
    s.gf[:, :, ROWS : ROWS + 8, :] = s.gfhalo[...]
    input_grads(s.gf, fw_ref, s.room, gproj_ref)
    each(tap_copy, lambda copy: copy.wait_recv())
    total = s.pk[ctx].astype(F32)
    for i in range(1, PEERS):
        total = total + s.rk[i].astype(F32)
    s.tot[...] = total.astype(BF16)
    s.fk[ctx] = s.tot[...]
    each(total_copy, lambda copy: copy.start())

    for copy in outs:
        copy.wait_recv()
    out_ref[:, z_cols(0)] = s.rb_own[...]
    for by, role in ((-way, "back"), (way, "fore"), (2, "far")):
        out_ref[:, z_cols(by)] = of("fin_", role)[...]

    each(total_copy, lambda copy: copy.wait_recv())
    norm = TOKENS**-0.5
    for q in range(PEERS):
        done = s.fk[q].astype(F32) * norm
        taps_ref[q * 8 : (q + 1) * 8, 0:512] = done[0:8, 0:512]
        taps_ref[q * 8 : (q + 1) * 8, 512:1024] = done[8:16, 0:512]
        if q < 9:
            for i in range(8):
                short_ref[q // 3, q % 3 : q % 3 + 1, i * 128 : (i + 1) * 128] = done[i : i + 1, 512:640]

    each(tap_copy, lambda copy: copy.wait_send())
    each(total_copy, lambda copy: copy.wait_send())
    for copy in started:
        copy.wait_send()


def hand_over(*refs):
    count = len(refs) // 2
    for i in range(count):
        refs[count + i][...] = refs[i][...]


def shards(projected, feat_weight, long_filter, out_weight, seg_lengths, cotangent):
    tab, tabt = (jnp.asarray(t) for t in tables())
    vm = pl.BlockSpec(memory_space=pltpu.VMEM)
    dma = pltpu.SemaphoreType.DMA
    outs = [
        jax.ShapeDtypeStruct((OWN, 4 * WIDE), BF16),
        jax.ShapeDtypeStruct((3, ROWS, CH), BF16),
        jax.ShapeDtypeStruct((128, CH), F32),
        jax.ShapeDtypeStruct((3, 3, CH), F32),
    ]
    results = pl.pallas_call(
        kernel,
        out_shape=outs,
        in_specs=[pl.BlockSpec(memory_space=pltpu.SMEM)] + [vm] * 7,
        out_specs=[vm] * 4,
        scratch_shapes=[pltpu.VMEM(shape, kind) for shape, kind in PLACES.values()]
        + [dma((SLOTS,)), dma((SLOTS,)), dma((PEERS,)), dma((PEERS,)), dma((PEERS,)), dma((PEERS,))],
        compiler_params=pltpu.CompilerParams(
            collective_id=0, has_side_effects=True, vmem_limit_bytes=60 * 2**20
        ),
    )(seg_lengths, projected, feat_weight, long_filter, out_weight, cotangent, tab, tabt)
    return tuple(
        pl.pallas_call(hand_over, out_shape=outs, in_specs=[vm] * 4, out_specs=[vm] * 4)(*results)
    )


def solution(mesh):
    return jax.shard_map(
        shards,
        mesh=mesh,
        in_specs=(
            P(None, "ctx", "tp"),
            P(None, None, "tp"),
            P(None, "tp"),
            P("tp", "ctx"),
            P(),
            P(("ctx", "tp"), None),
        ),
        out_specs=(
            P(("ctx", "tp"), None),
            P(None, "ctx", "tp"),
            P(None, "tp"),
            P(None, None, "tp"),
        ),
        check_vma=False,
    )
```

```python
import jax
import jax.numpy as jnp
import numpy as np
from jax import lax
from jax.experimental import pallas as pl
from jax.experimental.pallas import tpu as pltpu
from jax.sharding import PartitionSpec as P

F32 = jnp.float32
BF16 = jnp.bfloat16
ROWS = 256
CH = 1024
LB = CH // 128
BLK = 16
FAR = 8
TOKENS = 4096
NSEG = 32
PAD = 16
CHUNKS = 4
SPAN = LB // CHUNKS


def tables():
    turn = np.pi * (2 * np.arange(BLK) + 1) / (2 * BLK)

    def wave(at):
        return np.concatenate([np.cos(np.outer(turn, at)), -np.sin(np.outer(turn, at))])

    into = wave(np.arange(BLK))
    back = wave(np.arange(BLK) + BLK) / BLK
    back[BLK:] = -back[BLK:]
    taps = np.zeros((FAR * 2 * BLK, FAR * BLK))
    window = wave(np.arange(2 * BLK))
    for k in range(FAR):
        for d in range(1, 2 * BLK):
            if k * BLK + d < FAR * BLK:
                taps[k * 2 * BLK : (k + 1) * 2 * BLK, k * BLK + d] = window[:, d]
    each = np.eye(FAR)
    stack = np.stack([np.kron(each, into), np.kron(each, back), taps])
    return stack.astype(jnp.bfloat16), np.swapaxes(stack, 1, 2).astype(jnp.bfloat16)


def lanes(l):
    return pl.ds(pl.multiple_of(l * 128, 128), 128)


def rows_at(start, count):
    return pl.ds(pl.multiple_of(start, 8), count)


def find_ages(seg_ref, base, age_ref, room_ref):
    def chunk(i, carry):
        at = rows_at(i * 64, 64)
        pos = lax.broadcasted_iota(jnp.int32, (64, 128), 0) + (base - 128 + i * 64)

        def one(k, state):
            start, latest, after = state
            end = start + seg_ref[k]
            inside = pos >= start
            return end, jnp.where(inside, start, latest), jnp.where(inside, end, after)

        zero = jnp.zeros((64, 128), jnp.int32)
        _, latest, after = lax.fori_loop(0, NSEG, one, (jnp.int32(0), zero, zero))
        age_ref[at, :] = jnp.where(pos < TOKENS, pos - latest, -1)
        room_ref[at, :] = after - pos
        return carry

    lax.fori_loop(0, 8, chunk, 0)


def in_block(count):
    return lax.rem(lax.broadcasted_iota(jnp.int32, (count, 128), 0), BLK)


def load_inputs(source, pj, first, count):
    def lane(l, carry):
        for b in range(3):
            pj[b, l, first : first + count, :] = source[b, :, lanes(l)].astype(F32)
        return carry

    lax.fori_loop(0, LB, lane, 0)


def features(pj, fw_ref, age_ref, room_ref, feats, xs, xv, prod, first, count):
    def step(at, carry):
        l, r0 = at // count, (first + at % count) * 64
        age = age_ref[rows_at(128 + r0, 64), :]
        inside = in_block(64)
        got = []
        for b in range(3):
            total = pj[b, l, rows_at(PAD + r0, 64), :] * fw_ref[b, 0:1, lanes(l)]
            for i in range(1, 3):
                window = pj[b, l, pl.ds(PAD + r0 - i, 64), :]
                total = total + jnp.where(age >= i, window, 0.0) * fw_ref[b, i : i + 1, lanes(l)]
            feats[b, l, rows_at(r0, 64), :] = total
            got.append(total)
        product = (got[1] * got[2]).astype(BF16)
        wide = product.astype(F32)
        xs[l, rows_at(PAD + r0, 64), :] = wide
        live = room_ref[rows_at(128 + r0, 64), :] >= BLK - inside
        xv[pl.ds(pl.multiple_of(128 + r0, 16), 64), lanes(l)] = jnp.where(live, wide, 0.0).astype(BF16)
        if first:
            prod[pl.ds(pl.multiple_of(r0 - 128, 16), 64), lanes(l)] = product
        return carry

    lax.fori_loop(0, LB * count, step, 0)


def mask_halo(phalo_ref, room_ref, xv):
    def step(at, carry):
        l, r0 = at // 2, (at % 2) * 64
        live = room_ref[rows_at(r0, 64), :] >= BLK - in_block(64)
        rows = pl.ds(pl.multiple_of(r0, 16), 64)
        xv[rows, lanes(l)] = jnp.where(live, phalo_ref[rows, lanes(l)].astype(F32), 0.0).astype(BF16)
        return carry

    lax.fori_loop(0, LB * 2, step, 0)


def chunk_cols(c):
    return pl.ds(pl.multiple_of(c * 256, 256), 256)


def transform(table, source, target, group, c):
    target[group * 256 : (group + 1) * 256, chunk_cols(c)] = jnp.dot(
        table, source[group * 128 : (group + 1) * 128, chunk_cols(c)], preferred_element_type=F32
    )


def all_chunks(act):
    def step(c, carry):
        act(c)
        return carry

    lax.fori_loop(0, CHUNKS, step, 0)


GROUP = 16


def pair(ref, at, l, ft):
    base = at * 32 + ft * 8
    return ref[rows_at(base, 8), lanes(l)], ref[rows_at(base + 16, 8), lanes(l)]


def reach_of(age_ref, m):
    return jnp.broadcast_to(age_ref[pl.ds(128 + m * BLK - 1, 1), :], (8, 128))


def where_pair(live, value):
    return jnp.where(live, value[0], 0.0), jnp.where(live, value[1], 0.0)


def times(a, b):
    return a[0] * b[0] - a[1] * b[1], a[0] * b[1] + a[1] * b[0]


def far_forward(spec_x, spec_g, age_ref, spec_y):
    def outer(at, carry):
        l, ft = at // 2, at % 2
        g = [pair(spec_g, k, l, ft) for k in range(FAR)]

        def inner(q, carry):
            m0 = q * GROUP
            x = [pair(spec_x, m0 + i, l, ft) for i in range(FAR + GROUP - 1)]
            for m in range(GROUP):
                reach = reach_of(age_ref, m0 + m)
                terms = []
                for k in range(1, FAR + 1):
                    terms.append(times(g[k - 1], where_pair(reach >= BLK * (k - 1), x[FAR + m - k])))
                re = sum(t[0] for t in terms[1:]) + terms[0][0]
                im = sum(t[1] for t in terms[1:]) + terms[0][1]
                spec_y[rows_at((m0 + m) * 32 + ft * 8, 8), lanes(l)] = re
                spec_y[rows_at((m0 + m) * 32 + 16 + ft * 8, 8), lanes(l)] = -im
            return carry

        lax.fori_loop(0, ROWS // BLK // GROUP, inner, 0)
        return carry

    lax.fori_loop(0, LB * 2, outer, 0)


def far_back(spec_z, spec_g, age_ref, spec_p, c):
    def outer(at, carry):
        l, ft = c * SPAN + at // 2, at % 2
        g = [pair(spec_g, k, l, ft) for k in range(FAR)]

        def inner(q, carry):
            n0 = q * GROUP
            z = [pair(spec_z, n0 + 1 + i, l, ft) for i in range(FAR + GROUP - 1)]
            reach = [reach_of(age_ref, n0 + 1 + i) for i in range(FAR + GROUP - 1)]
            for n in range(GROUP):
                terms = []
                for k in range(1, FAR + 1):
                    terms.append(times(g[k - 1], where_pair(reach[n + k - 1] >= BLK * (k - 1), z[n + k - 1])))
                re = sum(t[0] for t in terms[1:]) + terms[0][0]
                im = sum(t[1] for t in terms[1:]) + terms[0][1]
                spec_p[rows_at((n0 + n) * 32 + ft * 8, 8), lanes(l)] = re
                spec_p[rows_at((n0 + n) * 32 + 16 + ft * 8, 8), lanes(l)] = -im
            return carry

        lax.fori_loop(0, ROWS // BLK // GROUP, inner, 0)
        return carry

    lax.fori_loop(0, SPAN * 2, outer, 0)


def far_taps(spec_x, spec_z, age_ref, spec_q, c):
    def outer(at, carry):
        l, ft = c * SPAN + at // 2, at % 2

        def inner(q, state):
            m0 = q * GROUP
            x = [pair(spec_x, m0 + i, l, ft) for i in range(FAR + GROUP - 1)]
            for m in range(GROUP):
                reach = reach_of(age_ref, m0 + m)
                z = pair(spec_z, m0 + m, l, ft)
                out = []
                for k in range(1, FAR + 1):
                    re, im = times(where_pair(reach >= BLK * (k - 1), x[FAR + m - k]), z)
                    out += [state[2 * k - 2] + re, state[2 * k - 1] + im]
                state = tuple(out)
            return state

        zero = jnp.zeros((8, 128), F32)
        state = lax.fori_loop(0, ROWS // BLK // GROUP, inner, (zero,) * (2 * FAR))
        for k in range(FAR):
            spec_q[rows_at(k * 32 + ft * 8, 8), lanes(l)] = state[2 * k]
            spec_q[rows_at(k * 32 + 16 + ft * 8, 8), lanes(l)] = -state[2 * k + 1]
        return carry

    lax.fori_loop(0, SPAN * 2, outer, 0)


def inverse(table, source, target, groups, c):
    for group in range(groups):
        target[group * 128 : (group + 1) * 128, chunk_cols(c)] = jnp.dot(
            table, source[group * 256 : (group + 1) * 256, chunk_cols(c)].astype(BF16), preferred_element_type=F32
        )


def near_forward(xs, lf_ref, age_ref, wide, feats, filt, gated):
    def step(at, carry):
        l, r0 = at // 4, (at % 4) * 64
        age = age_ref[rows_at(128 + r0, 64), :]
        inside = in_block(64)
        near = jnp.minimum(age, inside)
        total = jnp.where(age > inside, wide[rows_at(r0, 64), lanes(l)], 0.0)
        for j in range(BLK):
            window = xs[l, pl.ds(PAD + r0 - j, 64), :]
            total = total + jnp.where(near >= j, window, 0.0) * lf_ref[j : j + 1, lanes(l)]
        filt[l, rows_at(r0, 64), :] = total
        gate = feats[0, l, rows_at(r0, 64), :] * total
        gated[pl.ds(pl.multiple_of(r0, 16), 64), lanes(l)] = gate.astype(BF16)
        return carry

    lax.fori_loop(0, LB * 4, step, 0)


def make_long(gg_ref, feats, age_ref, gs_, gl, gv, c):
    def step(at, carry):
        lane, r0 = at // 4, (at % 4) * 64
        l = c * SPAN + lane
        rows = pl.ds(pl.multiple_of(r0, 16), 64)
        sent = (gg_ref[rows, lanes(l)].astype(F32) * feats[0, l, rows_at(r0, 64), :]).astype(BF16)
        long = sent.astype(F32)
        gl[rows, lanes(lane)] = sent
        gs_[l, rows_at(r0, 64), :] = long
        live = age_ref[rows_at(128 + r0, 64), :] > in_block(64)
        gv[rows, lanes(l)] = jnp.where(live, long, 0.0).astype(BF16)
        return carry

    lax.fori_loop(0, SPAN * 4, step, 0)


def mask_next(glhalo_ref, age_ref, gv, c):
    def step(at, carry):
        lane, r0 = at // 2, (at % 2) * 64
        live = age_ref[rows_at(128 + ROWS + r0, 64), :] > in_block(64)
        source = pl.ds(pl.multiple_of(r0, 16), 64)
        long = glhalo_ref[source, lanes(lane)].astype(F32)
        rows = pl.ds(pl.multiple_of(ROWS + r0, 16), 64)
        gv[rows, lanes(c * SPAN + lane)] = jnp.where(live, long, 0.0).astype(BF16)
        return carry

    lax.fori_loop(0, SPAN * 2, step, 0)


def near_back(gs_, xs, lf_ref, age_ref, room_ref, wide, gg_ref, filt, feats, gf, near_taps, c):
    def lane(at, carry):
        l = c * SPAN + at

        def step(i, sums):
            r0 = i * 64
            age = age_ref[rows_at(128 + r0, 64), :]
            room = room_ref[rows_at(128 + r0, 64), :]
            inside = in_block(64)
            near = jnp.minimum(age, inside)
            ahead = jnp.minimum(room, BLK - inside)
            here = gs_[l, rows_at(r0, 64), :]
            total = jnp.where(room >= BLK - inside, wide[rows_at(r0, 64), lanes(l)], 0.0)
            out = []
            for j in range(BLK):
                later = gs_[l, pl.ds(r0 + j, 64), :]
                total = total + jnp.where(ahead > j, later, 0.0) * lf_ref[j : j + 1, lanes(l)]
                window = xs[l, pl.ds(PAD + r0 - j, 64), :]
                both = jnp.where(near >= j, window, 0.0) * here
                out.append(sums[j] + jnp.sum(both.reshape(8, 8, 128), axis=0))
            grad = gg_ref[pl.ds(pl.multiple_of(r0, 16), 64), lanes(l)].astype(F32)
            gf[0, l, rows_at(r0, 64), :] = grad * filt[l, rows_at(r0, 64), :]
            gf[1, l, rows_at(r0, 64), :] = total * feats[2, l, rows_at(r0, 64), :]
            gf[2, l, rows_at(r0, 64), :] = total * feats[1, l, rows_at(r0, 64), :]
            return tuple(out)

        sums = lax.fori_loop(0, 4, step, (jnp.zeros((8, 128), F32),) * BLK)
        for j in range(BLK):
            near_taps[j : j + 1, lanes(l)] = jnp.sum(sums[j], axis=0, keepdims=True)
        return carry

    lax.fori_loop(0, SPAN, lane, 0)


def short_sums(gf, pj, age_ref, short, c):
    def lane(at_lane, carry):
        l = c * SPAN + at_lane

        def step(i, sums):
            r0 = i * 64
            age = age_ref[rows_at(128 + r0, 64), :]
            out = []
            for b in range(3):
                here = gf[b, l, rows_at(r0, 64), :]
                for tap in range(3):
                    window = pj[b, l, pl.ds(PAD + r0 - tap, 64), :]
                    if tap:
                        window = jnp.where(age >= tap, window, 0.0)
                    out.append(sums[b * 3 + tap] + jnp.sum((here * window).reshape(8, 8, 128), axis=0))
            return tuple(out)

        sums = lax.fori_loop(0, 4, step, (jnp.zeros((8, 128), F32),) * 9)
        for at in range(9):
            short[at : at + 1, lanes(l)] = jnp.sum(sums[at], axis=0, keepdims=True)
        return carry

    lax.fori_loop(0, SPAN, lane, 0)


def input_grads(gf, fw_ref, room_ref, gproj_ref, c):
    def step(at, carry):
        l, r0 = c * SPAN + at // 4, (at % 4) * 64
        room = room_ref[rows_at(128 + r0, 64), :]
        for b in range(3):
            total = gf[b, l, rows_at(r0, 64), :] * fw_ref[b, 0:1, lanes(l)]
            for tap in range(1, 3):
                later = gf[b, l, pl.ds(r0 + tap, 64), :]
                total = total + jnp.where(room > tap, later, 0.0) * fw_ref[b, tap : tap + 1, lanes(l)]
            gproj_ref[b, pl.ds(pl.multiple_of(r0, 16), 64), lanes(l)] = total.astype(BF16)
        return carry

    lax.fori_loop(0, SPAN * 4, step, 0)


MESH = pl.DeviceIdType.MESH
NX = 4
COLS = 384
WIDE = NX * COLS
OWN = 32
PEERS = 16


def turned(at, by):
    return lax.rem(at + by + 2 * NX, NX)


class Bag:
    pass


LANED = (LB, ROWS, 128)
PADDED = (LB, PAD + ROWS, 128)
SPEC = (3 * 256, CH)
AGE = (512, 128)
PART = (ROWS, CH // CHUNKS)
BLOCK = (OWN, WIDE)
ROLES = ("own", "back", "fore", "far")
PLACES = dict(
    pj=((3,) + PADDED, F32), feats=((3,) + LANED, F32), filt=(LANED, F32), xs=(PADDED, F32),
    xv=((128 + ROWS, CH), BF16), prod=((128, CH), BF16), jhalo=((3, 16, CH), BF16), phalo=((128, CH), BF16),
    age=(AGE, jnp.int32), room=(AGE, jnp.int32), lfb=((128, CH), BF16), spec_x=(SPEC, F32),
    spec_g=((256, CH), F32), spec_y=((512, CH), F32), wide=((ROWS, CH), F32), gs=(PADDED, F32),
    gv=((ROWS + 128, CH), BF16), spec_z=(SPEC, F32), spec_q=((256, CH), F32), gf=((3,) + PADDED, F32),
    taps=((128, CH), F32), near_taps=((BLK, CH), F32), short=((16, CH), F32),
    cg=((8, 4) + BLOCK, BF16), gg=((ROWS, CH), BF16),
)
for _h, _w in ((0, 256), (1, 384)):
    for _k in ("pk", "rk", "fk"):
        PLACES["%s%d" % (_k, _h)] = ((PEERS, 16, _w), BF16)
    PLACES["tot%d" % _h] = ((16, _w), BF16)
for _c in range(CHUNKS):
    PLACES["wg%d" % _c] = ((NX, CH // CHUNKS, COLS), BF16)
    PLACES["gl%d" % _c] = (PART, BF16)
    PLACES["glhalo%d" % _c] = ((128, CH // CHUNKS), BF16)
    PLACES["gfhalo%d" % _c] = ((3, SPAN, 8, 128), F32)
    for _r in ROLES:
        PLACES["part_%s%d" % (_r, _c)] = (PART, BF16)
    for _r in "abct":
        PLACES["rs_%s%d" % (_r, _c)] = (PART, BF16)
for _r in ROLES:
    PLACES["ga_" + _r] = ((ROWS, CH), BF16)
    PLACES["ob_" + _r] = ((4, 2) + BLOCK, BF16)
    PLACES["co_" + _r] = ((4,) + BLOCK, BF16)
    PLACES["sb_" + _r] = ((4,) + BLOCK, BF16)
    for _k in "abct":
        PLACES["y%s_%s" % (_k, _r)] = (BLOCK, BF16)
    PLACES["rb_" + _r] = (BLOCK, BF16)
    PLACES["fin_" + _r] = (BLOCK, BF16)
SLOTS = 96


def kernel(
    seg_ref, proj_ref, fw_ref, lf_ref, w_ref, cot_ref, tab_ref, tabt_ref,
    out_ref, gproj_ref, taps_ref, short_ref, *scratch,
):
    s = Bag()
    for name, ref in zip(PLACES, scratch):
        setattr(s, name, ref)
    send, recv, t_send, t_recv, u_send, u_recv = scratch[len(PLACES) :]

    def of(name, which):
        return getattr(s, name + str(which))

    ctx, tp = lax.axis_index("ctx"), lax.axis_index("tp")
    z, x, y, core = ctx // 4, ctx % 4, tp // 2, tp % 2
    way = 1 - 2 * core
    other = (ctx, y * 2 + (1 - core))

    def at_x(by):
        return (z * 4 + turned(x, by), tp)

    def at_z(by):
        return (turned(z, by) * 4 + x, tp)

    def at_y(by):
        return (ctx, turned(y, by) * 2 + core)

    def at_ctx(by):
        return (lax.rem(ctx + by + PEERS, PEERS), tp)

    barrier = pltpu.get_barrier_semaphore()
    for by in range(1, PEERS):
        pl.semaphore_signal(barrier, inc=1, device_id=at_ctx(by), device_id_type=MESH)
    for peer in (at_y(1), at_y(-1), other):
        pl.semaphore_signal(barrier, inc=1, device_id=peer, device_id_type=MESH)
    pl.semaphore_wait(barrier, PEERS + 2)

    started = []

    def remote(source, target, peer):
        slot = len(started)
        copy = pltpu.make_async_remote_copy(
            src_ref=source, dst_ref=target, send_sem=send.at[slot], recv_sem=recv.at[slot],
            device_id=peer, device_id_type=MESH,
        )
        copy.start()
        started.append(copy)
        return copy

    def z_cols(by):
        return pl.ds(pl.multiple_of(turned(z, by) * WIDE, 128), WIDE)

    def slab(by):
        return cg.at[turned(y, by) * 2 + core]

    def rest(by):
        return cg.at[turned(y, by) * 2 + core, pl.ds(1, 3)]

    cg = s.cg
    mine = cot_ref.at[:, z_cols(0)]
    c_ahead = remote(mine, cg.at[tp, 0], at_y(way))
    c_behind = remote(mine, cg.at[tp, 0], at_y(-way))
    cot_in = [remote(cot_ref.at[:, z_cols(by)], cg.at[tp, 4 - by], at_z(by)) for by in (1, 3, 2)]
    j_copy = remote(proj_ref.at[:, pl.ds(ROWS - 16, 16), :], s.jhalo, at_ctx(1))
    w_ahead, w_behind, w_on = [], [], []

    def w_send(c):
        rows = w_ref.at[pl.ds(c * 256, 256), :]
        w_ahead.append(remote(rows, of("wg", c).at[x], at_x(way)))
        w_behind.append(remote(rows, of("wg", c).at[x], at_x(-way)))

    def w_pass(c):
        w_ahead[c].wait_recv()
        passed = of("wg", c).at[turned(x, -way)]
        w_on.append(remote(passed, passed, at_x(way)))

    w_send(0)
    core_copies = [remote(mine, cg.at[tp, 0], other)]
    for c in range(CHUNKS):
        of("wg", c)[x] = w_ref[c * 256 : (c + 1) * 256, :]
    cg[tp, 0] = cot_ref[:, z_cols(0)]

    find_ages(seg_ref, ctx * ROWS, s.age, s.room)
    load_inputs(proj_ref, s.pj, PAD, ROWS)
    s.xs[:, 0:PAD, :] = jnp.zeros((LB, PAD, 128), F32)
    features(s.pj, fw_ref, s.age, s.room, s.feats, s.xs, s.xv, s.prod, 2, 2)
    p_copy = remote(s.prod, s.phalo, at_ctx(1))

    w_send(1)
    w_send(2)
    w_send(3)
    s.lfb[...] = lf_ref[...].astype(BF16)
    all_chunks(lambda c: transform(tab_ref[2], s.lfb, s.spec_g, 0, c))
    c_ahead.wait_recv()
    c_on = remote(cg.at[turned(y, -way) * 2 + core, 0], cg.at[turned(y, -way) * 2 + core, 0], at_y(way))
    for copy in cot_in:
        copy.wait_recv()
    d_ahead = remote(rest(0), rest(0), at_y(way))
    d_behind = remote(rest(0), rest(0), at_y(-way))
    core_copies.append(remote(rest(0), rest(0), other))

    j_copy.wait_recv()
    load_inputs(s.jhalo, s.pj, 0, PAD)
    features(s.pj, fw_ref, s.age, s.room, s.feats, s.xs, s.xv, s.prod, 0, 2)
    for group in (1, 2):
        all_chunks(lambda c, group=group: transform(tab_ref[0], s.xv, s.spec_x, group, c))

    p_copy.wait_recv()
    mask_halo(s.phalo, s.room, s.xv)
    all_chunks(lambda c: transform(tab_ref[0], s.xv, s.spec_x, 0, c))
    far_forward(s.spec_x, s.spec_g, s.age, s.spec_y)
    d_ahead.wait_recv()
    d_on = remote(rest(-way), rest(-way), at_y(way))
    core_copies.append(remote(slab(-way), slab(-way), other))
    all_chunks(lambda c: inverse(tabt_ref[1], s.spec_y, s.wide, 2, c))
    near_forward(s.xs, lf_ref, s.age, s.wide, s.feats, s.filt, s.ga_own)
    ga_ahead = remote(s.ga_own, s.ga_back, at_z(way))
    ga_behind = remote(s.ga_own, s.ga_fore, at_z(-way))

    for c in range(CHUNKS):
        w_pass(c)
    c_behind.wait_recv()
    d_behind.wait_recv()
    core_copies.append(remote(slab(way), slab(way), other))
    c_on.wait_recv()
    d_on.wait_recv()
    core_copies.append(remote(slab(2), slab(2), other))
    for copy in core_copies:
        copy.wait_recv()

    def backward_part(c, by, target):
        block = turned(0, by)
        total = jnp.zeros(PART, F32)
        for at in range(NX):
            total = total + lax.dot_general(
                cg[:, block, :, at * COLS : (at + 1) * COLS].reshape(ROWS, COLS), of("wg", c)[at],
                (((1,), (1,)), ((), ())), preferred_element_type=F32,
            )
        target[...] = total.astype(BF16)

    def add_rows(target, terms):
        def step(i, carry):
            rows = pl.ds(pl.multiple_of(i * 64, 64), 64)
            total = terms[0][rows, :].astype(F32)
            for term in terms[1:]:
                total = total + term[rows, :].astype(F32)
            target(rows, total.astype(BF16))
            return carry

        lax.fori_loop(0, ROWS // 64, step, 0)

    s_a, s_b, s_c = [], [], []
    for c in range(CHUNKS):
        w_behind[c].wait_recv()
        w_on[c].wait_recv()
        backward_part(c, 2, of("part_far", c))
        s_a.append(remote(of("part_far", c), of("rs_a", c), at_z(way)))
        backward_part(c, -way, of("part_back", c))
        s_b.append(remote(of("part_back", c), of("rs_b", c), at_z(-way)))
        backward_part(c, way, of("part_fore", c))
        backward_part(c, 0, of("part_own", c))

    def forward_part(rows, target):
        def step(at, carry):
            got = jnp.zeros((ROWS, COLS), F32)
            for c in range(CHUNKS):
                got = got + jnp.dot(
                    rows[:, c * 256 : (c + 1) * 256], of("wg", c)[at], preferred_element_type=F32
                )
            cols = pl.ds(pl.multiple_of(at * COLS, 128), COLS)
            target[:, :, :, cols] = got.astype(BF16).reshape(4, 2, OWN, COLS)
            return carry

        lax.fori_loop(0, NX, step, 0)

    there = dict(own="own", back="fore", fore="back", far="far")
    o_core, y_copies, outs = {}, {}, []

    def forward_role(role):
        forward_part(of("ga_", role), of("ob_", role))
        o_core[role] = remote(of("ob_", role).at[:, 1 - core], of("co_", there[role]), other)

    def y_first(role):
        o_core[there[role]].wait_recv()
        ob, co, sb = of("ob_", role), of("co_", role), of("sb_", role)

        def step(q, carry):
            sb[q] = (ob[q, core].astype(F32) + co[q].astype(F32)).astype(BF16)
            return carry

        lax.fori_loop(0, 4, step, 0)
        y_copies[role] = [
            remote(sb.at[turned(y, 2)], of("ya_", role), at_y(way)),
            remote(sb.at[turned(y, -way)], of("yb_", role), at_y(-way)),
        ]

    def y_second(role):
        y_copies[role][0].wait_recv()
        held = of("yt_", role)
        held[...] = (of("ya_", role)[...].astype(F32) + of("sb_", role)[turned(y, way)].astype(F32)).astype(BF16)
        y_copies[role].append(remote(held, of("yc_", role), at_y(way)))

    def y_last(role):
        y_copies[role][1].wait_recv()
        y_copies[role][2].wait_recv()
        total = of("sb_", role)[y].astype(F32) + of("yb_", role)[...].astype(F32) + of("yc_", role)[...].astype(F32)
        of("rb_", role)[...] = total.astype(BF16)
        if role != "own":
            by = dict(back=-way, fore=way, far=2)[role]
            outs.append(remote(of("rb_", role), of("fin_", there[role]), at_z(by)))

    forward_role("own")
    for c in range(CHUNKS):
        s_a[c].wait_recv()
        held = of("rs_t", c)

        def put(rows, value, held=held):
            held[rows, :] = value

        add_rows(put, (of("rs_a", c), of("part_fore", c)))
        s_c.append(remote(held, of("rs_c", c), at_z(way)))
    ga_ahead.wait_recv()
    ga_on = remote(s.ga_back, s.ga_far, at_z(way))
    forward_role("back")
    ga_behind.wait_recv()
    forward_role("fore")
    y_first("own")

    l_copies = []
    s.gs[:, ROWS : ROWS + PAD, :] = jnp.zeros((LB, PAD, 128), F32)

    def back_first(c):
        s_b[c].wait_recv()
        s_c[c].wait_recv()

        def put(rows, value):
            s.gg[rows, c * 256 : (c + 1) * 256] = value

        add_rows(put, (of("part_own", c), of("rs_b", c), of("rs_c", c)))
        make_long(s.gg, s.feats, s.age, s.gs, of("gl", c), s.gv, c)
        l_copies.append(remote(of("gl", c).at[pl.ds(0, 128), :], of("glhalo", c), at_ctx(-1)))
        for group in (0, 1):
            transform(tab_ref[1], s.gv, s.spec_z, group, c)
        far_taps(s.spec_x, s.spec_z, s.age, s.spec_q, c)

    f_copies = []

    def back_second(c):
        l_copies[c].wait_recv()
        mask_next(of("glhalo", c), s.age, s.gv, c)
        transform(tab_ref[1], s.gv, s.spec_z, 2, c)
        far_back(s.spec_z, s.spec_g, s.age, s.spec_y, c)
        inverse(tabt_ref[0], s.spec_y, s.wide, 2, c)
        near_back(
            s.gs, s.xs, lf_ref, s.age, s.room, s.wide, s.gg, s.filt, s.feats, s.gf, s.near_taps, c
        )
        f_copies.append(
            remote(s.gf.at[:, pl.ds(c * SPAN, SPAN), pl.ds(0, 8), :], of("gfhalo", c), at_ctx(-1))
        )
        inverse(tabt_ref[2], s.spec_q, s.taps, 1, c)
        cols = pl.ds(c * 256, 256)
        s.taps[0:BLK, cols] = s.taps[0:BLK, cols] + s.near_taps[:, cols]
        short_sums(s.gf, s.pj, s.age, s.short, c)

    def back_third(c):
        f_copies[c].wait_recv()
        s.gf[:, c * SPAN : (c + 1) * SPAN, ROWS : ROWS + 8, :] = of("gfhalo", c)[...]
        input_grads(s.gf, fw_ref, s.room, gproj_ref, c)

    def pack(h):
        pk = of("pk", h)
        for q in range(PEERS):
            rows = s.taps[q * 8 : (q + 1) * 8, h * 512 : (h + 1) * 512]
            pk[q, :, 0:256] = jnp.concatenate([rows[:, 0:256], rows[:, 256:512]], axis=0).astype(BF16)
            if h and q < 9:
                row = [s.short[q : q + 1, i * 128 : (i + 1) * 128] for i in range(8)]
                row.append(jnp.zeros((8, 128), F32))
                pk[q, :, 256:384] = jnp.concatenate(row, axis=0).astype(BF16)
            elif h:
                pk[q, :, 256:384] = jnp.zeros((16, 128), BF16)

    def tap_copy(h):
        def make(i):
            peer = lax.rem(ctx + i, PEERS)
            return pltpu.make_async_remote_copy(
                src_ref=of("pk", h).at[peer], dst_ref=of("rk", h).at[i], send_sem=t_send.at[h, i],
                recv_sem=t_recv.at[h, i], device_id=(peer, tp), device_id_type=MESH,
            )

        return make

    def total_copy(h):
        def make(i):
            peer = lax.rem(ctx + i, PEERS)
            return pltpu.make_async_remote_copy(
                src_ref=of("tot", h), dst_ref=of("fk", h).at[ctx], send_sem=u_send.at[h, i],
                recv_sem=u_recv.at[h, i], device_id=(peer, tp), device_id_type=MESH,
            )

        return make

    def each(make, act):
        def step(i, carry):
            act(make(i))
            return carry

        lax.fori_loop(1, PEERS, step, 0)

    def send_taps(h):
        pack(h)
        each(tap_copy(h), lambda copy: copy.start())

    def sum_taps(h):
        each(tap_copy(h), lambda copy: copy.wait_recv())
        total = of("pk", h)[ctx].astype(F32)
        for i in range(1, PEERS):
            total = total + of("rk", h)[i].astype(F32)
        of("tot", h)[...] = total.astype(BF16)
        of("fk", h)[ctx] = of("tot", h)[...]
        each(total_copy(h), lambda copy: copy.start())

    def finish_taps(h):
        each(total_copy(h), lambda copy: copy.wait_recv())
        norm = TOKENS**-0.5
        for q in range(PEERS):
            done = of("fk", h)[q].astype(F32) * norm
            taps_ref[q * 8 : (q + 1) * 8, h * 512 : h * 512 + 256] = done[0:8, 0:256]
            taps_ref[q * 8 : (q + 1) * 8, h * 512 + 256 : (h + 1) * 512] = done[8:16, 0:256]
            if h and q < 9:
                for i in range(8):
                    short_ref[q // 3, q % 3 : q % 3 + 1, i * 128 : (i + 1) * 128] = done[i : i + 1, 256:384]

    back_first(0)
    y_first("back")
    y_first("fore")
    y_second("own")
    back_first(1)
    ga_on.wait_recv()
    forward_role("far")
    y_second("back")
    y_second("fore")
    back_second(0)
    back_first(2)
    y_first("far")
    y_last("own")
    back_second(1)
    send_taps(0)
    y_last("back")
    y_last("fore")
    back_first(3)
    y_second("far")
    back_second(2)
    sum_taps(0)
    back_third(0)
    y_last("far")
    back_second(3)
    send_taps(1)
    back_third(1)
    finish_taps(0)
    for copy in outs:
        copy.wait_recv()
    out_ref[:, z_cols(0)] = s.rb_own[...]
    for by, role in ((-way, "back"), (way, "fore"), (2, "far")):
        out_ref[:, z_cols(by)] = of("fin_", role)[...]
    sum_taps(1)
    back_third(2)
    back_third(3)
    finish_taps(1)

    for h in range(2):
        each(tap_copy(h), lambda copy: copy.wait_send())
        each(total_copy(h), lambda copy: copy.wait_send())
    for copy in started:
        copy.wait_send()


def hand_over(*refs):
    count = len(refs) // 2
    for i in range(count):
        refs[count + i][...] = refs[i][...]


def shards(projected, feat_weight, long_filter, out_weight, seg_lengths, cotangent):
    tab, tabt = (jnp.asarray(t) for t in tables())
    vm = pl.BlockSpec(memory_space=pltpu.VMEM)
    dma = pltpu.SemaphoreType.DMA
    outs = [
        jax.ShapeDtypeStruct((OWN, 4 * WIDE), BF16),
        jax.ShapeDtypeStruct((3, ROWS, CH), BF16),
        jax.ShapeDtypeStruct((128, CH), F32),
        jax.ShapeDtypeStruct((3, 3, CH), F32),
    ]
    results = pl.pallas_call(
        kernel,
        out_shape=outs,
        in_specs=[pl.BlockSpec(memory_space=pltpu.SMEM)] + [vm] * 7,
        out_specs=[vm] * 4,
        scratch_shapes=[pltpu.VMEM(shape, kind) for shape, kind in PLACES.values()]
        + [dma((SLOTS,)), dma((SLOTS,)), *[dma((2, PEERS))] * 4],
        compiler_params=pltpu.CompilerParams(
            collective_id=0, has_side_effects=True, vmem_limit_bytes=60 * 2**20
        ),
    )(seg_lengths, projected, feat_weight, long_filter, out_weight, cotangent, tab, tabt)
    return tuple(
        pl.pallas_call(hand_over, out_shape=outs, in_specs=[vm] * 4, out_specs=[vm] * 4)(*results)
    )


def solution(mesh):
    return jax.shard_map(
        shards,
        mesh=mesh,
        in_specs=(
            P(None, "ctx", "tp"),
            P(None, None, "tp"),
            P(None, "tp"),
            P("tp", "ctx"),
            P(),
            P(("ctx", "tp"), None),
        ),
        out_specs=(
            P(("ctx", "tp"), None),
            P(None, "ctx", "tp"),
            P(None, "tp"),
            P(None, None, "tp"),
        ),
        check_vma=False,
    )
```

```python
import jax
import jax.numpy as jnp
import numpy as np
from jax import lax
from jax.experimental import pallas as pl
from jax.experimental.pallas import tpu as pltpu
from jax.sharding import PartitionSpec as P

F32 = jnp.float32
BF16 = jnp.bfloat16
ROWS = 256
CH = 1024
LB = CH // 128
BLK = 16
FAR = 8
TOKENS = 4096
NSEG = 32
PAD = 16
CHUNKS = 4
SPAN = LB // CHUNKS


def tables():
    turn = np.pi * (2 * np.arange(BLK) + 1) / (2 * BLK)

    def wave(at):
        return np.concatenate([np.cos(np.outer(turn, at)), -np.sin(np.outer(turn, at))])

    into = wave(np.arange(BLK))
    back = wave(np.arange(BLK) + BLK) / BLK
    back[BLK:] = -back[BLK:]
    taps = np.zeros((FAR * 2 * BLK, FAR * BLK))
    window = wave(np.arange(2 * BLK))
    for k in range(FAR):
        for d in range(1, 2 * BLK):
            if k * BLK + d < FAR * BLK:
                taps[k * 2 * BLK : (k + 1) * 2 * BLK, k * BLK + d] = window[:, d]
    each = np.eye(FAR)
    stack = np.stack([np.kron(each, into), np.kron(each, back), taps])
    return stack.astype(jnp.bfloat16), np.swapaxes(stack, 1, 2).astype(jnp.bfloat16)


def lanes(l):
    return pl.ds(pl.multiple_of(l * 128, 128), 128)


def rows_at(start, count):
    return pl.ds(pl.multiple_of(start, 8), count)


def find_ages(seg_ref, base, age_ref, room_ref, first, last):
    def chunk(i, carry):
        at = rows_at(i * 64, 64)
        pos = lax.broadcasted_iota(jnp.int32, (64, 128), 0) + (base - 128 + i * 64)

        def one(k, state):
            start, latest, after = state
            end = start + seg_ref[k]
            inside = pos >= start
            return end, jnp.where(inside, start, latest), jnp.where(inside, end, after)

        zero = jnp.zeros((64, 128), jnp.int32)
        _, latest, after = lax.fori_loop(0, NSEG, one, (jnp.int32(0), zero, zero))
        age_ref[at, :] = jnp.where(pos < TOKENS, pos - latest, -1)
        room_ref[at, :] = after - pos
        return carry

    lax.fori_loop(first, last, chunk, 0)


def in_block(count):
    return lax.rem(lax.broadcasted_iota(jnp.int32, (count, 128), 0), BLK)


def load_inputs(source, pj, first, count, start=0):
    def lane(l, carry):
        for b in range(3):
            pj[b, l, first : first + count, :] = source[b, start : start + count, lanes(l)].astype(F32)
        return carry

    lax.fori_loop(0, LB, lane, 0)


def features(pj, fw_ref, age_ref, room_ref, feats, xs, xv, prod, first, count):
    def step(at, carry):
        l, r0 = at // count, (first + at % count) * 64
        age = age_ref[rows_at(128 + r0, 64), :]
        inside = in_block(64)
        got = []
        for b in range(3):
            total = pj[b, l, rows_at(PAD + r0, 64), :] * fw_ref[b, 0:1, lanes(l)]
            for i in range(1, 3):
                window = pj[b, l, pl.ds(PAD + r0 - i, 64), :]
                total = total + jnp.where(age >= i, window, 0.0) * fw_ref[b, i : i + 1, lanes(l)]
            feats[b, l, rows_at(r0, 64), :] = total
            got.append(total)
        product = (got[1] * got[2]).astype(BF16)
        wide = product.astype(F32)
        xs[l, rows_at(PAD + r0, 64), :] = wide
        live = room_ref[rows_at(128 + r0, 64), :] >= BLK - inside
        xv[pl.ds(pl.multiple_of(128 + r0, 16), 64), lanes(l)] = jnp.where(live, wide, 0.0).astype(BF16)
        if first:
            prod[pl.ds(pl.multiple_of(r0 - 128, 16), 64), lanes(l)] = product
        return carry

    lax.fori_loop(0, LB * count, step, 0)


def mask_halo(phalo_ref, room_ref, xv):
    def step(at, carry):
        l, r0 = at // 2, (at % 2) * 64
        live = room_ref[rows_at(r0, 64), :] >= BLK - in_block(64)
        rows = pl.ds(pl.multiple_of(r0, 16), 64)
        xv[rows, lanes(l)] = jnp.where(live, phalo_ref[rows, lanes(l)].astype(F32), 0.0).astype(BF16)
        return carry

    lax.fori_loop(0, LB * 2, step, 0)


def chunk_cols(c):
    return pl.ds(pl.multiple_of(c * 256, 256), 256)


def transform(table, source, target, group, c):
    target[group * 256 : (group + 1) * 256, chunk_cols(c)] = jnp.dot(
        table, source[group * 128 : (group + 1) * 128, chunk_cols(c)], preferred_element_type=F32
    )


def all_chunks(act):
    def step(c, carry):
        act(c)
        return carry

    lax.fori_loop(0, CHUNKS, step, 0)


GROUP = 16


def pair(ref, at, l, ft):
    base = at * 32 + ft * 8
    return ref[rows_at(base, 8), lanes(l)], ref[rows_at(base + 16, 8), lanes(l)]


def reach_of(age_ref, m):
    return jnp.broadcast_to(age_ref[pl.ds(128 + m * BLK - 1, 1), :], (8, 128))


def where_pair(live, value):
    return jnp.where(live, value[0], 0.0), jnp.where(live, value[1], 0.0)


def times(a, b):
    return a[0] * b[0] - a[1] * b[1], a[0] * b[1] + a[1] * b[0]


def far_forward(spec_x, spec_g, age_ref, spec_y):
    def outer(at, carry):
        l, ft = at // 2, at % 2
        g = [pair(spec_g, k, l, ft) for k in range(FAR)]

        def inner(q, carry):
            m0 = q * GROUP
            x = [pair(spec_x, m0 + i, l, ft) for i in range(FAR + GROUP - 1)]
            for m in range(GROUP):
                reach = reach_of(age_ref, m0 + m)
                terms = []
                for k in range(1, FAR + 1):
                    terms.append(times(g[k - 1], where_pair(reach >= BLK * (k - 1), x[FAR + m - k])))
                re = sum(t[0] for t in terms[1:]) + terms[0][0]
                im = sum(t[1] for t in terms[1:]) + terms[0][1]
                spec_y[rows_at((m0 + m) * 32 + ft * 8, 8), lanes(l)] = re
                spec_y[rows_at((m0 + m) * 32 + 16 + ft * 8, 8), lanes(l)] = -im
            return carry

        lax.fori_loop(0, ROWS // BLK // GROUP, inner, 0)
        return carry

    lax.fori_loop(0, LB * 2, outer, 0)


def far_back(spec_z, spec_g, age_ref, spec_p, c):
    def outer(at, carry):
        l, ft = c * SPAN + at // 2, at % 2
        g = [pair(spec_g, k, l, ft) for k in range(FAR)]

        def inner(q, carry):
            n0 = q * GROUP
            z = [pair(spec_z, n0 + 1 + i, l, ft) for i in range(FAR + GROUP - 1)]
            reach = [reach_of(age_ref, n0 + 1 + i) for i in range(FAR + GROUP - 1)]
            for n in range(GROUP):
                terms = []
                for k in range(1, FAR + 1):
                    terms.append(times(g[k - 1], where_pair(reach[n + k - 1] >= BLK * (k - 1), z[n + k - 1])))
                re = sum(t[0] for t in terms[1:]) + terms[0][0]
                im = sum(t[1] for t in terms[1:]) + terms[0][1]
                spec_p[rows_at((n0 + n) * 32 + ft * 8, 8), lanes(l)] = re
                spec_p[rows_at((n0 + n) * 32 + 16 + ft * 8, 8), lanes(l)] = -im
            return carry

        lax.fori_loop(0, ROWS // BLK // GROUP, inner, 0)
        return carry

    lax.fori_loop(0, SPAN * 2, outer, 0)


def far_taps(spec_x, spec_z, age_ref, spec_q, c):
    def outer(at, carry):
        l, ft = c * SPAN + at // 2, at % 2

        def inner(q, state):
            m0 = q * GROUP
            x = [pair(spec_x, m0 + i, l, ft) for i in range(FAR + GROUP - 1)]
            for m in range(GROUP):
                reach = reach_of(age_ref, m0 + m)
                z = pair(spec_z, m0 + m, l, ft)
                out = []
                for k in range(1, FAR + 1):
                    re, im = times(where_pair(reach >= BLK * (k - 1), x[FAR + m - k]), z)
                    out += [state[2 * k - 2] + re, state[2 * k - 1] + im]
                state = tuple(out)
            return state

        zero = jnp.zeros((8, 128), F32)
        state = lax.fori_loop(0, ROWS // BLK // GROUP, inner, (zero,) * (2 * FAR))
        for k in range(FAR):
            spec_q[rows_at(k * 32 + ft * 8, 8), lanes(l)] = state[2 * k]
            spec_q[rows_at(k * 32 + 16 + ft * 8, 8), lanes(l)] = -state[2 * k + 1]
        return carry

    lax.fori_loop(0, SPAN * 2, outer, 0)


def inverse(table, source, target, groups, c):
    for group in range(groups):
        target[group * 128 : (group + 1) * 128, chunk_cols(c)] = jnp.dot(
            table, source[group * 256 : (group + 1) * 256, chunk_cols(c)].astype(BF16), preferred_element_type=F32
        )


def near_forward(xs, lf_ref, age_ref, wide, feats, filt, gated):
    def step(at, carry):
        l, r0 = at // 4, (at % 4) * 64
        age = age_ref[rows_at(128 + r0, 64), :]
        inside = in_block(64)
        near = jnp.minimum(age, inside)
        total = jnp.where(age > inside, wide[rows_at(r0, 64), lanes(l)], 0.0)
        for j in range(BLK):
            window = xs[l, pl.ds(PAD + r0 - j, 64), :]
            total = total + jnp.where(near >= j, window, 0.0) * lf_ref[j : j + 1, lanes(l)]
        filt[l, rows_at(r0, 64), :] = total
        gate = feats[0, l, rows_at(r0, 64), :] * total
        gated[pl.ds(pl.multiple_of(r0, 16), 64), lanes(l)] = gate.astype(BF16)
        return carry

    lax.fori_loop(0, LB * 4, step, 0)


def make_long(gg_ref, feats, age_ref, gs_, gl, gv, c):
    def step(at, carry):
        lane, r0 = at // 4, (at % 4) * 64
        l = c * SPAN + lane
        rows = pl.ds(pl.multiple_of(r0, 16), 64)
        sent = (gg_ref[rows, lanes(l)].astype(F32) * feats[0, l, rows_at(r0, 64), :]).astype(BF16)
        long = sent.astype(F32)
        gl[rows, lanes(lane)] = sent
        gs_[l, rows_at(r0, 64), :] = long
        live = age_ref[rows_at(128 + r0, 64), :] > in_block(64)
        gv[rows, lanes(l)] = jnp.where(live, long, 0.0).astype(BF16)
        return carry

    lax.fori_loop(0, SPAN * 4, step, 0)


def mask_next(glhalo_ref, age_ref, gv, c):
    def step(at, carry):
        lane, r0 = at // 2, (at % 2) * 64
        live = age_ref[rows_at(128 + ROWS + r0, 64), :] > in_block(64)
        source = pl.ds(pl.multiple_of(r0, 16), 64)
        long = glhalo_ref[source, lanes(lane)].astype(F32)
        rows = pl.ds(pl.multiple_of(ROWS + r0, 16), 64)
        gv[rows, lanes(c * SPAN + lane)] = jnp.where(live, long, 0.0).astype(BF16)
        return carry

    lax.fori_loop(0, SPAN * 2, step, 0)


def near_back(gs_, xs, lf_ref, age_ref, room_ref, wide, gg_ref, filt, feats, gf, near_taps, c):
    def lane(at, carry):
        l = c * SPAN + at

        def step(i, sums):
            r0 = i * 64
            age = age_ref[rows_at(128 + r0, 64), :]
            room = room_ref[rows_at(128 + r0, 64), :]
            inside = in_block(64)
            near = jnp.minimum(age, inside)
            ahead = jnp.minimum(room, BLK - inside)
            here = gs_[l, rows_at(r0, 64), :]
            total = jnp.where(room >= BLK - inside, wide[rows_at(r0, 64), lanes(l)], 0.0)
            out = []
            for j in range(BLK):
                later = gs_[l, pl.ds(r0 + j, 64), :]
                total = total + jnp.where(ahead > j, later, 0.0) * lf_ref[j : j + 1, lanes(l)]
                window = xs[l, pl.ds(PAD + r0 - j, 64), :]
                both = jnp.where(near >= j, window, 0.0) * here
                out.append(sums[j] + jnp.sum(both.reshape(8, 8, 128), axis=0))
            grad = gg_ref[pl.ds(pl.multiple_of(r0, 16), 64), lanes(l)].astype(F32)
            gf[0, l, rows_at(r0, 64), :] = grad * filt[l, rows_at(r0, 64), :]
            gf[1, l, rows_at(r0, 64), :] = total * feats[2, l, rows_at(r0, 64), :]
            gf[2, l, rows_at(r0, 64), :] = total * feats[1, l, rows_at(r0, 64), :]
            return tuple(out)

        sums = lax.fori_loop(0, 4, step, (jnp.zeros((8, 128), F32),) * BLK)
        for j in range(BLK):
            near_taps[j : j + 1, lanes(l)] = jnp.sum(sums[j], axis=0, keepdims=True)
        return carry

    lax.fori_loop(0, SPAN, lane, 0)


def short_sums(gf, pj, age_ref, short, c):
    def lane(at_lane, carry):
        l = c * SPAN + at_lane

        def step(i, sums):
            r0 = i * 64
            age = age_ref[rows_at(128 + r0, 64), :]
            out = []
            for b in range(3):
                here = gf[b, l, rows_at(r0, 64), :]
                for tap in range(3):
                    window = pj[b, l, pl.ds(PAD + r0 - tap, 64), :]
                    if tap:
                        window = jnp.where(age >= tap, window, 0.0)
                    out.append(sums[b * 3 + tap] + jnp.sum((here * window).reshape(8, 8, 128), axis=0))
            return tuple(out)

        sums = lax.fori_loop(0, 4, step, (jnp.zeros((8, 128), F32),) * 9)
        for at in range(9):
            short[at : at + 1, lanes(l)] = jnp.sum(sums[at], axis=0, keepdims=True)
        return carry

    lax.fori_loop(0, SPAN, lane, 0)


def input_grads(gf, fw_ref, room_ref, gproj_ref, c):
    def step(at, carry):
        l, r0 = c * SPAN + at // 4, (at % 4) * 64
        room = room_ref[rows_at(128 + r0, 64), :]
        for b in range(3):
            total = gf[b, l, rows_at(r0, 64), :] * fw_ref[b, 0:1, lanes(l)]
            for tap in range(1, 3):
                later = gf[b, l, pl.ds(r0 + tap, 64), :]
                total = total + jnp.where(room > tap, later, 0.0) * fw_ref[b, tap : tap + 1, lanes(l)]
            gproj_ref[b, pl.ds(pl.multiple_of(r0, 16), 64), lanes(l)] = total.astype(BF16)
        return carry

    lax.fori_loop(0, SPAN * 4, step, 0)


MESH = pl.DeviceIdType.MESH
NX = 4
COLS = 384
WIDE = NX * COLS
OWN = 32
PEERS = 16


def turned(at, by):
    return lax.rem(at + by + 2 * NX, NX)


class Bag:
    pass


LANED = (LB, ROWS, 128)
PADDED = (LB, PAD + ROWS, 128)
SPEC = (3 * 256, CH)
AGE = (512, 128)
PART = (ROWS, CH // CHUNKS)
BLOCK = (OWN, WIDE)
ROLES = ("own", "back", "fore", "far")
PLACES = dict(
    pj=((3,) + PADDED, F32), feats=((3,) + LANED, F32), filt=(LANED, F32), xs=(PADDED, F32),
    xv=((128 + ROWS, CH), BF16), prod=((128, CH), BF16), jhalo=((3, 16, CH), BF16), phalo=((128, CH), BF16),
    age=(AGE, jnp.int32), room=(AGE, jnp.int32), lfb=((128, CH), BF16), spec_x=(SPEC, F32),
    spec_g=((256, CH), F32), spec_y=((512, CH), F32), wide=((ROWS, CH), F32), gs=(PADDED, F32),
    gv=((ROWS + 128, CH), BF16), spec_z=(SPEC, F32), spec_q=((256, CH), F32), gf=((3,) + PADDED, F32),
    taps=((128, CH), F32), near_taps=((BLK, CH), F32), short=((16, CH), F32),
    cg=((8, 4) + BLOCK, BF16), gg=((ROWS, CH), BF16),
)
for _h, _w in ((0, 256), (1, 384)):
    for _k in ("pk", "rk", "fk"):
        PLACES["%s%d" % (_k, _h)] = ((PEERS, 16, _w), BF16)
    PLACES["tot%d" % _h] = ((16, _w), BF16)
for _c in range(CHUNKS):
    PLACES["wg%d" % _c] = ((NX, CH // CHUNKS, COLS), BF16)
    PLACES["gl%d" % _c] = (PART, BF16)
    PLACES["glhalo%d" % _c] = ((128, CH // CHUNKS), BF16)
    PLACES["gfhalo%d" % _c] = ((3, SPAN, 8, 128), F32)
    for _r in ROLES:
        PLACES["part_%s%d" % (_r, _c)] = (PART, BF16)
    for _r in "abct":
        PLACES["rs_%s%d" % (_r, _c)] = (PART, BF16)
for _r in ROLES:
    PLACES["ga_" + _r] = ((ROWS, CH), BF16)
    PLACES["ob_" + _r] = ((4, 2) + BLOCK, BF16)
    PLACES["co_" + _r] = ((4,) + BLOCK, BF16)
    PLACES["sb_" + _r] = ((4,) + BLOCK, BF16)
    for _k in "abct":
        PLACES["y%s_%s" % (_k, _r)] = (BLOCK, BF16)
    PLACES["rb_" + _r] = (BLOCK, BF16)
    PLACES["fin_" + _r] = (BLOCK, BF16)
SLOTS = 96


def kernel(
    seg_ref, proj_ref, fw_ref, lf_ref, w_ref, cot_ref, tab_ref, tabt_ref,
    out_ref, gproj_ref, taps_ref, short_ref, *scratch,
):
    s = Bag()
    for name, ref in zip(PLACES, scratch):
        setattr(s, name, ref)
    send, recv, t_send, t_recv, u_send, u_recv = scratch[len(PLACES) :]

    def of(name, which):
        return getattr(s, name + str(which))

    ctx, tp = lax.axis_index("ctx"), lax.axis_index("tp")
    z, x, y, core = ctx // 4, ctx % 4, tp // 2, tp % 2
    way = 1 - 2 * core
    other = (ctx, y * 2 + (1 - core))

    def at_x(by):
        return (z * 4 + turned(x, by), tp)

    def at_z(by):
        return (turned(z, by) * 4 + x, tp)

    def at_y(by):
        return (ctx, turned(y, by) * 2 + core)

    def at_ctx(by):
        return (lax.rem(ctx + by + PEERS, PEERS), tp)

    barrier = pltpu.get_barrier_semaphore()
    for by in range(1, PEERS):
        pl.semaphore_signal(barrier, inc=1, device_id=at_ctx(by), device_id_type=MESH)
    for peer in (at_y(1), at_y(-1), other):
        pl.semaphore_signal(barrier, inc=1, device_id=peer, device_id_type=MESH)
    pl.semaphore_wait(barrier, PEERS + 2)

    started = []

    def remote(source, target, peer):
        slot = len(started)
        copy = pltpu.make_async_remote_copy(
            src_ref=source, dst_ref=target, send_sem=send.at[slot], recv_sem=recv.at[slot],
            device_id=peer, device_id_type=MESH,
        )
        copy.start()
        started.append(copy)
        return copy

    def z_cols(by):
        return pl.ds(pl.multiple_of(turned(z, by) * WIDE, 128), WIDE)

    def slab(by):
        return cg.at[turned(y, by) * 2 + core]

    def rest(by):
        return cg.at[turned(y, by) * 2 + core, pl.ds(1, 3)]

    cg = s.cg
    mine = cot_ref.at[:, z_cols(0)]
    c_ahead = remote(mine, cg.at[tp, 0], at_y(way))
    c_behind = remote(mine, cg.at[tp, 0], at_y(-way))
    cot_in = [remote(cot_ref.at[:, z_cols(by)], cg.at[tp, 4 - by], at_z(by)) for by in (1, 3, 2)]
    j_copy = remote(proj_ref.at[:, pl.ds(ROWS - 16, 16), :], s.jhalo, at_ctx(1))
    w_ahead, w_behind, w_on = [], [], []

    def w_send(c):
        rows = w_ref.at[pl.ds(c * 256, 256), :]
        w_ahead.append(remote(rows, of("wg", c).at[x], at_x(way)))
        w_behind.append(remote(rows, of("wg", c).at[x], at_x(-way)))

    def w_pass(c):
        w_ahead[c].wait_recv()
        passed = of("wg", c).at[turned(x, -way)]
        w_on.append(remote(passed, passed, at_x(way)))

    w_send(0)
    core_copies = [remote(mine, cg.at[tp, 0], other)]

    find_ages(seg_ref, ctx * ROWS, s.age, s.room, 4, 6)
    load_inputs(proj_ref, s.pj, PAD + 112, ROWS - 112, 112)
    features(s.pj, fw_ref, s.age, s.room, s.feats, s.xs, s.xv, s.prod, 2, 2)
    p_copy = remote(s.prod, s.phalo, at_ctx(1))

    w_send(1)
    w_send(2)
    w_send(3)
    for c in range(CHUNKS):
        of("wg", c)[x] = w_ref[c * 256 : (c + 1) * 256, :]
    cg[tp, 0] = cot_ref[:, z_cols(0)]
    find_ages(seg_ref, ctx * ROWS, s.age, s.room, 0, 4)
    find_ages(seg_ref, ctx * ROWS, s.age, s.room, 6, 8)
    load_inputs(proj_ref, s.pj, PAD, 112)
    s.xs[:, 0:PAD, :] = jnp.zeros((LB, PAD, 128), F32)
    s.lfb[...] = lf_ref[...].astype(BF16)
    all_chunks(lambda c: transform(tab_ref[2], s.lfb, s.spec_g, 0, c))
    c_ahead.wait_recv()
    c_on = remote(cg.at[turned(y, -way) * 2 + core, 0], cg.at[turned(y, -way) * 2 + core, 0], at_y(way))
    for copy in cot_in:
        copy.wait_recv()
    d_ahead = remote(rest(0), rest(0), at_y(way))
    d_behind = remote(rest(0), rest(0), at_y(-way))
    core_copies.append(remote(rest(0), rest(0), other))

    j_copy.wait_recv()
    load_inputs(s.jhalo, s.pj, 0, PAD)
    features(s.pj, fw_ref, s.age, s.room, s.feats, s.xs, s.xv, s.prod, 0, 2)
    for group in (1, 2):
        all_chunks(lambda c, group=group: transform(tab_ref[0], s.xv, s.spec_x, group, c))

    p_copy.wait_recv()
    mask_halo(s.phalo, s.room, s.xv)
    all_chunks(lambda c: transform(tab_ref[0], s.xv, s.spec_x, 0, c))
    far_forward(s.spec_x, s.spec_g, s.age, s.spec_y)
    d_ahead.wait_recv()
    d_on = remote(rest(-way), rest(-way), at_y(way))
    core_copies.append(remote(slab(-way), slab(-way), other))
    all_chunks(lambda c: inverse(tabt_ref[1], s.spec_y, s.wide, 2, c))
    near_forward(s.xs, lf_ref, s.age, s.wide, s.feats, s.filt, s.ga_own)
    ga_ahead = remote(s.ga_own, s.ga_back, at_z(way))
    ga_behind = remote(s.ga_own, s.ga_fore, at_z(-way))

    for c in range(CHUNKS):
        w_pass(c)
    c_behind.wait_recv()
    d_behind.wait_recv()
    core_copies.append(remote(slab(way), slab(way), other))
    c_on.wait_recv()
    d_on.wait_recv()
    core_copies.append(remote(slab(2), slab(2), other))
    for copy in core_copies:
        copy.wait_recv()

    def backward_part(c, by, target):
        block = turned(0, by)
        total = jnp.zeros(PART, F32)
        for at in range(NX):
            total = total + lax.dot_general(
                cg[:, block, :, at * COLS : (at + 1) * COLS].reshape(ROWS, COLS), of("wg", c)[at],
                (((1,), (1,)), ((), ())), preferred_element_type=F32,
            )
        target[...] = total.astype(BF16)

    def add_rows(target, terms):
        def step(i, carry):
            rows = pl.ds(pl.multiple_of(i * 64, 64), 64)
            total = terms[0][rows, :].astype(F32)
            for term in terms[1:]:
                total = total + term[rows, :].astype(F32)
            target(rows, total.astype(BF16))
            return carry

        lax.fori_loop(0, ROWS // 64, step, 0)

    def reduce_on(c):
        s_a[c].wait_recv()
        held = of("rs_t", c)

        def put(rows, value, held=held):
            held[rows, :] = value

        add_rows(put, (of("rs_a", c), of("part_fore", c)))
        s_c.append(remote(held, of("rs_c", c), at_z(way)))

    s_a, s_b, s_c = [], [], []
    for c in range(CHUNKS):
        w_behind[c].wait_recv()
        w_on[c].wait_recv()
        backward_part(c, 2, of("part_far", c))
        s_a.append(remote(of("part_far", c), of("rs_a", c), at_z(way)))
        backward_part(c, -way, of("part_back", c))
        s_b.append(remote(of("part_back", c), of("rs_b", c), at_z(-way)))
        backward_part(c, way, of("part_fore", c))
        backward_part(c, 0, of("part_own", c))
        if c >= 2:
            reduce_on(c - 2)

    def forward_part(rows, target):
        def step(at, carry):
            got = jnp.zeros((ROWS, COLS), F32)
            for c in range(CHUNKS):
                got = got + jnp.dot(
                    rows[:, c * 256 : (c + 1) * 256], of("wg", c)[at], preferred_element_type=F32
                )
            cols = pl.ds(pl.multiple_of(at * COLS, 128), COLS)
            target[:, :, :, cols] = got.astype(BF16).reshape(4, 2, OWN, COLS)
            return carry

        lax.fori_loop(0, NX, step, 0)

    there = dict(own="own", back="fore", fore="back", far="far")
    o_core, y_copies, outs = {}, {}, []

    def forward_role(role):
        forward_part(of("ga_", role), of("ob_", role))
        o_core[role] = remote(of("ob_", role).at[:, 1 - core], of("co_", there[role]), other)

    def y_first(role):
        o_core[there[role]].wait_recv()
        ob, co, sb = of("ob_", role), of("co_", role), of("sb_", role)

        def step(q, carry):
            sb[q] = (ob[q, core].astype(F32) + co[q].astype(F32)).astype(BF16)
            return carry

        lax.fori_loop(0, 4, step, 0)
        y_copies[role] = [
            remote(sb.at[turned(y, 2)], of("ya_", role), at_y(way)),
            remote(sb.at[turned(y, -way)], of("yb_", role), at_y(-way)),
        ]

    def y_second(role):
        y_copies[role][0].wait_recv()
        held = of("yt_", role)
        held[...] = (of("ya_", role)[...].astype(F32) + of("sb_", role)[turned(y, way)].astype(F32)).astype(BF16)
        y_copies[role].append(remote(held, of("yc_", role), at_y(way)))

    def y_last(role):
        y_copies[role][1].wait_recv()
        y_copies[role][2].wait_recv()
        total = of("sb_", role)[y].astype(F32) + of("yb_", role)[...].astype(F32) + of("yc_", role)[...].astype(F32)
        of("rb_", role)[...] = total.astype(BF16)
        if role != "own":
            by = dict(back=-way, fore=way, far=2)[role]
            outs.append(remote(of("rb_", role), of("fin_", there[role]), at_z(by)))

    forward_role("own")
    for c in (2, 3):
        reduce_on(c)
    ga_ahead.wait_recv()
    ga_on = remote(s.ga_back, s.ga_far, at_z(way))
    forward_role("back")
    ga_behind.wait_recv()
    forward_role("fore")
    y_first("own")

    l_copies = []
    s.gs[:, ROWS : ROWS + PAD, :] = jnp.zeros((LB, PAD, 128), F32)

    def back_first(c):
        s_b[c].wait_recv()
        s_c[c].wait_recv()

        def put(rows, value):
            s.gg[rows, c * 256 : (c + 1) * 256] = value

        add_rows(put, (of("part_own", c), of("rs_b", c), of("rs_c", c)))
        make_long(s.gg, s.feats, s.age, s.gs, of("gl", c), s.gv, c)
        l_copies.append(remote(of("gl", c).at[pl.ds(0, 128), :], of("glhalo", c), at_ctx(-1)))
        for group in (0, 1):
            transform(tab_ref[1], s.gv, s.spec_z, group, c)
        far_taps(s.spec_x, s.spec_z, s.age, s.spec_q, c)

    f_copies = []

    def back_second(c):
        l_copies[c].wait_recv()
        mask_next(of("glhalo", c), s.age, s.gv, c)
        transform(tab_ref[1], s.gv, s.spec_z, 2, c)
        far_back(s.spec_z, s.spec_g, s.age, s.spec_y, c)
        inverse(tabt_ref[0], s.spec_y, s.wide, 2, c)
        near_back(
            s.gs, s.xs, lf_ref, s.age, s.room, s.wide, s.gg, s.filt, s.feats, s.gf, s.near_taps, c
        )
        f_copies.append(
            remote(s.gf.at[:, pl.ds(c * SPAN, SPAN), pl.ds(0, 8), :], of("gfhalo", c), at_ctx(-1))
        )
        inverse(tabt_ref[2], s.spec_q, s.taps, 1, c)
        cols = pl.ds(c * 256, 256)
        s.taps[0:BLK, cols] = s.taps[0:BLK, cols] + s.near_taps[:, cols]
        short_sums(s.gf, s.pj, s.age, s.short, c)

    def back_third(c):
        f_copies[c].wait_recv()
        s.gf[:, c * SPAN : (c + 1) * SPAN, ROWS : ROWS + 8, :] = of("gfhalo", c)[...]
        input_grads(s.gf, fw_ref, s.room, gproj_ref, c)

    def pack(h):
        pk = of("pk", h)
        for q in range(PEERS):
            rows = s.taps[q * 8 : (q + 1) * 8, h * 512 : (h + 1) * 512]
            pk[q, :, 0:256] = jnp.concatenate([rows[:, 0:256], rows[:, 256:512]], axis=0).astype(BF16)
            if h and q < 9:
                row = [s.short[q : q + 1, i * 128 : (i + 1) * 128] for i in range(8)]
                row.append(jnp.zeros((8, 128), F32))
                pk[q, :, 256:384] = jnp.concatenate(row, axis=0).astype(BF16)
            elif h:
                pk[q, :, 256:384] = jnp.zeros((16, 128), BF16)

    def tap_copy(h):
        def make(i):
            peer = lax.rem(ctx + i, PEERS)
            return pltpu.make_async_remote_copy(
                src_ref=of("pk", h).at[peer], dst_ref=of("rk", h).at[i], send_sem=t_send.at[h, i],
                recv_sem=t_recv.at[h, i], device_id=(peer, tp), device_id_type=MESH,
            )

        return make

    def total_copy(h):
        def make(i):
            peer = lax.rem(ctx + i, PEERS)
            return pltpu.make_async_remote_copy(
                src_ref=of("tot", h), dst_ref=of("fk", h).at[ctx], send_sem=u_send.at[h, i],
                recv_sem=u_recv.at[h, i], device_id=(peer, tp), device_id_type=MESH,
            )

        return make

    def each(make, act):
        def step(i, carry):
            act(make(i))
            return carry

        lax.fori_loop(1, PEERS, step, 0)

    def send_taps(h):
        pack(h)
        each(tap_copy(h), lambda copy: copy.start())

    def sum_taps(h):
        each(tap_copy(h), lambda copy: copy.wait_recv())
        total = of("pk", h)[ctx].astype(F32)
        for i in range(1, PEERS):
            total = total + of("rk", h)[i].astype(F32)
        of("tot", h)[...] = total.astype(BF16)
        of("fk", h)[ctx] = of("tot", h)[...]
        each(total_copy(h), lambda copy: copy.start())

    def finish_taps(h):
        each(total_copy(h), lambda copy: copy.wait_recv())
        norm = TOKENS**-0.5
        for q in range(PEERS):
            done = of("fk", h)[q].astype(F32) * norm
            taps_ref[q * 8 : (q + 1) * 8, h * 512 : h * 512 + 256] = done[0:8, 0:256]
            taps_ref[q * 8 : (q + 1) * 8, h * 512 + 256 : (h + 1) * 512] = done[8:16, 0:256]
            if h and q < 9:
                for i in range(8):
                    short_ref[q // 3, q % 3 : q % 3 + 1, i * 128 : (i + 1) * 128] = done[i : i + 1, 256:384]

    back_first(0)
    y_first("back")
    y_first("fore")
    y_second("own")
    back_first(1)
    ga_on.wait_recv()
    forward_role("far")
    y_second("back")
    y_second("fore")
    back_second(0)
    back_first(2)
    y_first("far")
    y_last("own")
    back_second(1)
    send_taps(0)
    y_last("back")
    y_last("fore")
    back_first(3)
    y_second("far")
    back_second(2)
    sum_taps(0)
    back_third(0)
    y_last("far")
    back_second(3)
    send_taps(1)
    back_third(1)
    finish_taps(0)
    for copy in outs:
        copy.wait_recv()
    out_ref[:, z_cols(0)] = s.rb_own[...]
    for by, role in ((-way, "back"), (way, "fore"), (2, "far")):
        out_ref[:, z_cols(by)] = of("fin_", role)[...]
    sum_taps(1)
    back_third(2)
    back_third(3)
    finish_taps(1)

    for h in range(2):
        each(tap_copy(h), lambda copy: copy.wait_send())
        each(total_copy(h), lambda copy: copy.wait_send())
    for copy in started:
        copy.wait_send()


def hand_over(*refs):
    sources, targets, held, sem = refs[0:4], refs[4:8], refs[8:12], refs[12]
    pieces = [(0, None), (2, None), (3, None)] + [(1, b) for b in range(3)]

    def part(ref, at):
        return ref if at is None else ref.at[at]

    into = [
        pltpu.make_async_copy(part(sources[i], at), part(held[i], at), sem.at[0, n]) for n, (i, at) in enumerate(pieces)
    ]
    back = [
        pltpu.make_async_copy(part(held[i], at), part(targets[i], at), sem.at[1, n]) for n, (i, at) in enumerate(pieces)
    ]
    for copy in into:
        copy.start()
    for n, copy in enumerate(into):
        copy.wait()
        back[n].start()
    for copy in back:
        copy.wait()


def shards(projected, feat_weight, long_filter, out_weight, seg_lengths, cotangent):
    tab, tabt = (jnp.asarray(t) for t in tables())
    vm = pl.BlockSpec(memory_space=pltpu.VMEM)
    dma = pltpu.SemaphoreType.DMA
    outs = [
        jax.ShapeDtypeStruct((OWN, 4 * WIDE), BF16),
        jax.ShapeDtypeStruct((3, ROWS, CH), BF16),
        jax.ShapeDtypeStruct((128, CH), F32),
        jax.ShapeDtypeStruct((3, 3, CH), F32),
    ]
    results = pl.pallas_call(
        kernel,
        out_shape=outs,
        in_specs=[pl.BlockSpec(memory_space=pltpu.SMEM)] + [vm] * 7,
        out_specs=[vm] * 4,
        scratch_shapes=[pltpu.VMEM(shape, kind) for shape, kind in PLACES.values()]
        + [dma((SLOTS,)), dma((SLOTS,)), *[dma((2, PEERS))] * 4],
        compiler_params=pltpu.CompilerParams(
            collective_id=0, has_side_effects=True, vmem_limit_bytes=60 * 2**20
        ),
    )(seg_lengths, projected, feat_weight, long_filter, out_weight, cotangent, tab, tabt)
    anywhere = pl.BlockSpec(memory_space=pl.ANY)
    return tuple(
        pl.pallas_call(
            hand_over,
            out_shape=outs,
            in_specs=[anywhere] * 4,
            out_specs=[anywhere] * 4,
            scratch_shapes=[pltpu.VMEM(o.shape, o.dtype) for o in outs] + [dma((2, 6))],
        )(*results)
    )


def solution(mesh):
    return jax.shard_map(
        shards,
        mesh=mesh,
        in_specs=(
            P(None, "ctx", "tp"),
            P(None, None, "tp"),
            P(None, "tp"),
            P("tp", "ctx"),
            P(),
            P(("ctx", "tp"), None),
        ),
        out_specs=(
            P(("ctx", "tp"), None),
            P(None, "ctx", "tp"),
            P(None, "tp"),
            P(None, None, "tp"),
        ),
        check_vma=False,
    )
```
